256 devices in a mesh: ctx: 16 (over z, core), exp: 16 (over y, x).
Axes of the slice: x: 4, y: 4, z: 8, core: 2. Of those that a mesh axis runs over, the one named last changes fastest.
Arguments:
- grad_out: bfloat16 [16, 2048, 4096], P('exp', 'ctx'), may hold values from -1.796875 to 1.796875
- routes: int32 [16, 2048, 1], P('exp', 'ctx'), may hold values from 0 to 15; in each aligned block of 128 rows (0 to 127, 128 to 255, ..., all dimensions but the last counted through in order) at most 12 rows name the same one
- gate_probs: float32 [16, 2048, 1], P('exp', 'ctx'), may hold values from 0.2 to 1
- saved_pre: bfloat16 [16, 16, 192, 1536], P('ctx', 'exp'), may hold values from -6 to 6
- down_weight: bfloat16 [16, 768, 4096], P('exp', None, 'ctx'), may hold values from -0.21875 to 0.21875
- gate_up_weight: bfloat16 [16, 4096, 1536], P('exp', 'ctx'), may hold values from -0.21875 to 0.21875
- queries: bfloat16 [16, 2048, 4096], P('exp', 'ctx')
- keys_values: bfloat16 [16, 2048, 512], P('exp', 'ctx')
- attn_grad: bfloat16 [16, 2048, 4096], P('exp', 'ctx'), may hold values from -6 to 6
- attn_out: bfloat16 [16, 2048, 4096], P('exp', 'ctx'), may hold values from -6 to 6
Outputs:
- moe_input_grad: bfloat16 [16, 2048, 4096], P('exp', 'ctx')
- prob_grad: bfloat16 [16, 2048, 1], P('exp', 'ctx')
- query_grad: bfloat16 [16, 2048, 4096], P('exp', 'ctx')
- kv_grad: bfloat16 [16, 2048, 512], P('exp', 'ctx')
The draws below stay inside these ranges and needn't reach their ends.
Inputs may be any that keep to these rules, and one draw needn't show every extreme that they name: `routes`: in the rows of one device no expert is named by more than 12 tokens, a bound that some block reaches.
All inputs are finite; a program needn't handle non-finite values.
Results may differ from the reference program's by a relative error of at most 0.0065.
Values may be sent and summed in bfloat16 or wider, within the bound.
No kernel may reach another device: no remote copies, remote signals or barrier semaphores. Data moves between devices by JAX's collectives and lax.ppermute only.
A program may use at most 192 MiB of HBM per device.

```python
import math
import jax
import jax.numpy as jnp
import numpy as np
from jax import lax

D = 4096
FFW = 768
QUERY_HEAD_COUNT = 32
KEY_VALUE_HEADS = 2
HEAD_SIZE = 128
TOPK = 1
TOK_DEV = 128
EXPERTS = 16
SEQUENCE_COUNT = 16
SEQUENCE_LENGTH = 2048
CAP = 12
N_CTX = 16
N_EXP = 16


def shared_keys(key):
    starting_keys = jax.random.normal(key, (SEQUENCE_COUNT, SEQUENCE_LENGTH, KEY_VALUE_HEADS, HEAD_SIZE), jnp.float32)
    anchor = jnp.arange(40, SEQUENCE_LENGTH, 53)
    blended = starting_keys[:, anchor - 17]
    return starting_keys.at[:, anchor - 17].set(blended)


def draw_keys_values(key, part):
    key_rows = shared_keys(key)
    key = jax.random.fold_in(key, 7)
    value_tensor = jax.random.normal(key, (SEQUENCE_COUNT, SEQUENCE_LENGTH, KEY_VALUE_HEADS, HEAD_SIZE), jnp.float32)
    joined_parts = jnp.concatenate([key_rows, value_tensor], axis=-1)
    return joined_parts.reshape(SEQUENCE_COUNT, SEQUENCE_LENGTH, KEY_VALUE_HEADS * 2 * HEAD_SIZE).astype(jnp.bfloat16)


def draw_queries(key, part):
    key = jax.random.fold_in(key, 5)
    queries = jax.random.normal(key, (SEQUENCE_COUNT, SEQUENCE_LENGTH, QUERY_HEAD_COUNT, HEAD_SIZE), jnp.float32)
    return queries.reshape(SEQUENCE_COUNT, SEQUENCE_LENGTH, QUERY_HEAD_COUNT * HEAD_SIZE).astype(jnp.bfloat16)


def level_of(stream_key, dims, shards, smallest, high):
    factor_of, own = 1.0, jax.random.fold_in(stream_key, 6)
    for dim, parts in shards:
        steps = jnp.exp(jax.random.uniform(jax.random.fold_in(own, dim), (parts,), jnp.float32, smallest / len(shards), high / len(shards)))
        factor_of = factor_of * jnp.repeat(steps, dims[dim] // parts).reshape([-1 if axis == dim else 1 for axis in range(len(dims))])
    return factor_of


def assign_block(stream_key, own, number, rows, count, top, most, lean):
    sequence = jax.random.permutation(stream_key, count)
    heavy_load, common = shares(count, rows * top, most, lean, True), shares(count, rows * top, most, lean, False)
    places = jnp.arange(count)

    def named(tallies, offset_by):
        used = int((tallies > 0).sum())
        fixed = max(1, used // 4)
        shifted = fixed + (places - fixed + offset_by * (used - fixed)) % max(1, count - fixed)
        return jnp.zeros((count,), jnp.int32).at[sequence[jnp.where(places < fixed, places, shifted)]].set(jnp.asarray(tallies, jnp.int32))

    tallies = jnp.where(number % 4 == 0, named(heavy_load, number // 4), named(common, number - number // 4 - 1))
    mixed = jax.random.permutation(jax.random.fold_in(own, 3), count)
    donor, receiver = mixed[0:count // 2 * 2:2], mixed[1:count // 2 * 2:2]
    slack = jnp.minimum(tallies[donor] - 1, most - tallies[receiver]) // 2
    slack = jnp.where((donor == sequence[0]) | (receiver == sequence[0]) | (tallies[receiver] == 0), 0, jnp.maximum(slack, 0))
    shifted = jax.random.randint(jax.random.fold_in(own, 4), (count // 2,), 0, 1 << 20) % (slack + 1)
    tallies = tallies.at[donor].add(-shifted).at[receiver].add(shifted)
    members = jnp.searchsorted(jnp.cumsum(tallies), jnp.arange(rows * top), side="right").astype(jnp.int32)
    listing = members.reshape(top, rows).T
    listing = listing[jax.random.permutation(jax.random.fold_in(own, 1), rows)]
    offset_by = jax.random.randint(jax.random.fold_in(own, 2), (rows, 1), 0, top)
    return jnp.take_along_axis(listing, (jnp.arange(top)[None, :] + offset_by) % top, axis=1)


def shares(count, total, bound, lean, full):
    weights = [(1 << 20) // math.isqrt(rank ** lean) + 1 for rank in range(1, count + 1)]
    largest = bound if full else min(bound, max(-(-total // count), total * weights[0] // sum(weights)))
    least = 1 if total - largest >= count - 1 else 0
    counts, spare = [largest] + [least] * (count - 1), total - largest - least * (count - 1)
    while spare > 0:
        movable = [i for i in range(1, count) if counts[i] < largest] or [i for i in range(1, count) if counts[i] < bound]
        pool, budget = sum([weights[i] for i in movable]), spare
        for i in movable:
            addition = min(bound - counts[i], max(1, budget * weights[i] // pool), spare)
            counts[i] = counts[i] + addition
            spare = spare - addition
    return np.array(counts)


def centred(stream_key, shape, spread, bound, split=(), held_as=jnp.bfloat16):
    values = jax.random.normal(stream_key, shape, jnp.float32) * spread
    if len(split) > 0:
        values = level_of(stream_key, shape, split, -0.22, 0.18) * values
    return jnp.clip(values, min=-bound, max=bound).astype(held_as)


def setup_inputs(seed: int = 0) -> dict:
    keys = jax.random.split(jax.random.key(seed), 11)
    grad_out = centred(keys[0], (SEQUENCE_COUNT, SEQUENCE_LENGTH, D), 0.3, 1.796875, ((0, 16), (1, 16)))
    routes_keys = jax.random.split(jax.random.fold_in(keys[1], 1), SEQUENCE_COUNT * SEQUENCE_LENGTH // TOK_DEV)
    routes_turns = jax.random.permutation(jax.random.fold_in(keys[1], 3), SEQUENCE_COUNT * SEQUENCE_LENGTH // TOK_DEV)
    routes = jax.vmap(lambda own, number: assign_block(jax.random.fold_in(keys[1], 2), own, number, TOK_DEV, EXPERTS, TOPK, CAP, 2))(routes_keys, routes_turns).reshape((SEQUENCE_COUNT, SEQUENCE_LENGTH, TOPK))
    gate_probs = jnp.clip(0.2 + 0.8 * jax.random.uniform(keys[2], (SEQUENCE_COUNT, SEQUENCE_LENGTH, TOPK), jnp.float32) ** level_of(keys[2], (SEQUENCE_COUNT, SEQUENCE_LENGTH, TOPK), ((0, 16), (1, 16)), -0.2, 0.2), 0.2, 1.0)
    saved_pre = centred(keys[3], (N_CTX, EXPERTS, N_EXP * CAP, 2 * FFW), 1.0, 6.0, ((0, 16), (1, 16)))
    down_weight = centred(keys[4], (EXPERTS, FFW, D), FFW ** -0.5, 0.21875, ((0, 16), (2, 16)))
    gate_up_weight = centred(keys[5], (EXPERTS, D, 2 * FFW), FFW ** -0.5, 0.21875, ((0, 16), (1, 16)))
    queries = draw_queries(jax.random.fold_in(keys[10], 71), 0)
    keys_values = draw_keys_values(jax.random.fold_in(keys[10], 71), 0)
    attn_grad = centred(keys[8], (SEQUENCE_COUNT, SEQUENCE_LENGTH, QUERY_HEAD_COUNT * HEAD_SIZE), 1.0, 6.0, ((0, 16), (1, 16)))
    attn_out = centred(keys[9], (SEQUENCE_COUNT, SEQUENCE_LENGTH, QUERY_HEAD_COUNT * HEAD_SIZE), 1.0, 6.0, ((0, 16), (1, 16)))
    return {"grad_out": grad_out, "routes": routes, "gate_probs": gate_probs, "saved_pre": saved_pre, "down_weight": down_weight, "gate_up_weight": gate_up_weight, "queries": queries, "keys_values": keys_values, "attn_grad": attn_grad, "attn_out": attn_out}


def slot_table(route_grid):
    flat_routes = route_grid.reshape(N_EXP, N_CTX, TOK_DEV * TOPK)
    one_hot = (flat_routes[..., None] == jnp.arange(EXPERTS, dtype=jnp.int32)).astype(jnp.int32)
    earlier = jnp.cumsum(one_hot, axis=2) - one_hot
    positions = jnp.sum(earlier * one_hot, axis=-1)
    return positions.reshape(N_EXP, N_CTX, TOK_DEV, TOPK).astype(jnp.int32)


def expert_backward(expert_rows, pre_acts, down_block, gate_up_block):
    down_grad = jnp.dot(expert_rows, down_block.T, preferred_element_type=jnp.float32)
    gate_pre = pre_acts[:, :FFW].astype(jnp.float32)
    up_pre = pre_acts[:, FFW:].astype(jnp.float32)
    sigma = jax.nn.sigmoid(gate_pre)
    swish = gate_pre * sigma
    slot_prob = jnp.sum(down_grad * swish * up_pre, axis=-1).astype(jnp.bfloat16)
    gate_part = down_grad * up_pre * sigma * (1.0 + gate_pre * (1.0 - sigma))
    up_part = down_grad * swish
    pre_grad = jnp.concatenate([gate_part, up_part], axis=-1).astype(jnp.bfloat16)
    slot_input = jnp.dot(pre_grad, gate_up_block.T, preferred_element_type=jnp.float32).astype(jnp.bfloat16)
    return slot_input, slot_prob


def moe_backward(grad_out, routes, gate_probs, saved_pre, down_weight, gate_up_weight):
    route_grid = routes.reshape(N_EXP, N_CTX, TOK_DEV, TOPK)
    prob_grid = gate_probs.reshape(N_EXP, N_CTX, TOK_DEV, TOPK)
    grad_grid = grad_out.reshape(N_EXP, N_CTX, TOK_DEV, D)
    positions = slot_table(route_grid)
    padded = jnp.concatenate([grad_grid, jnp.zeros((N_EXP, N_CTX, 1, D), grad_grid.dtype)], axis=2)
    shape_four = (N_EXP, N_CTX, TOK_DEV, TOPK)
    source_ids = jnp.broadcast_to(jnp.arange(N_EXP, dtype=jnp.int32)[:, None, None, None], shape_four)
    block_ids = jnp.broadcast_to(jnp.arange(N_CTX, dtype=jnp.int32)[None, :, None, None], shape_four)
    token_ids = jnp.broadcast_to(jnp.arange(TOK_DEV, dtype=jnp.int32)[None, None, :, None], shape_four)
    table = jnp.full((N_EXP, N_CTX, EXPERTS, CAP), TOK_DEV, jnp.int32)
    table = table.at[source_ids, block_ids, route_grid, positions].set(token_ids)

    def per_expert(carry, expert):
        input_acc, prob_acc = carry
        lookup = table[:, :, expert, :]
        gathered = jnp.take_along_axis(padded, lookup[..., None], axis=2)
        expert_rows = jnp.transpose(gathered, (1, 0, 2, 3)).reshape(N_CTX * N_EXP * CAP, D)
        pre_acts = saved_pre[:, expert].reshape(N_CTX * N_EXP * CAP, 2 * FFW)
        slot_input, slot_prob = expert_backward(expert_rows, pre_acts, down_weight[expert], gate_up_weight[expert])
        input_grid = jnp.transpose(slot_input.reshape(N_CTX, N_EXP, CAP, D), (1, 0, 2, 3))
        slot_grid = jnp.transpose(slot_prob.reshape(N_CTX, N_EXP, CAP), (1, 0, 2))
        for which in range(TOPK):
            chosen = route_grid[..., which] == expert
            slot_here = positions[..., which]
            picked = jnp.take_along_axis(input_grid, slot_here[..., None], axis=2)
            weight_here = jnp.where(chosen, prob_grid[..., which], jnp.float32(0.0))
            input_acc = input_acc + weight_here[..., None] * picked.astype(jnp.float32)
            prob_pick = jnp.take_along_axis(slot_grid, slot_here, axis=2).astype(jnp.float32)
            prob_acc = prob_acc.at[..., which].add(jnp.where(chosen, prob_pick, jnp.float32(0.0)))
        return (input_acc, prob_acc), None

    start_carry = (jnp.zeros((N_EXP, N_CTX, TOK_DEV, D), jnp.float32),
                   jnp.zeros((N_EXP, N_CTX, TOK_DEV, TOPK), jnp.float32))
    (input_acc, prob_acc), unused = lax.scan(per_expert, start_carry, jnp.arange(EXPERTS, dtype=jnp.int32))
    moe_input_grad = input_acc.astype(jnp.bfloat16).reshape(SEQUENCE_COUNT, SEQUENCE_LENGTH, D)
    prob_grad = prob_acc.astype(jnp.bfloat16).reshape(SEQUENCE_COUNT, SEQUENCE_LENGTH, TOPK)
    return moe_input_grad, prob_grad


def head_backward(items):
    query, grad_head, out_head, key_rows, value_rows = items
    scale = HEAD_SIZE ** -0.5
    scores = jnp.dot(query, key_rows.T, preferred_element_type=jnp.float32) * scale
    causal = jnp.arange(SEQUENCE_LENGTH)[:, None] >= jnp.arange(SEQUENCE_LENGTH)[None, :]
    scores = jnp.where(causal, scores, jnp.float32(-1e30))
    highest = jnp.max(scores, axis=-1, keepdims=True)
    expo = jnp.exp(scores - highest)
    probs = expo / jnp.sum(expo, axis=-1, keepdims=True)
    low_probs = probs.astype(jnp.bfloat16)
    value_grad = jnp.dot(low_probs.T, grad_head, preferred_element_type=jnp.float32)
    prob_part = jnp.dot(grad_head, value_rows.T, preferred_element_type=jnp.float32)
    delta = jnp.sum(grad_head.astype(jnp.float32) * out_head.astype(jnp.float32), axis=-1, keepdims=True)
    score_grad = (probs * (prob_part - delta)).astype(jnp.bfloat16)
    query_part = jnp.dot(score_grad, key_rows, preferred_element_type=jnp.float32) * scale
    key_portion = jnp.dot(score_grad.T, query, preferred_element_type=jnp.float32) * scale
    return query_part, key_portion, value_grad


def sequence_backward(items):
    query_seq, grad_seq, out_seq, key_value_sequence = items
    query_group = QUERY_HEAD_COUNT // KEY_VALUE_HEADS
    query_heads = jnp.transpose(query_seq.reshape(SEQUENCE_LENGTH, QUERY_HEAD_COUNT, HEAD_SIZE), (1, 0, 2))
    grad_heads = jnp.transpose(grad_seq.reshape(SEQUENCE_LENGTH, QUERY_HEAD_COUNT, HEAD_SIZE), (1, 0, 2))
    out_heads = jnp.transpose(out_seq.reshape(SEQUENCE_LENGTH, QUERY_HEAD_COUNT, HEAD_SIZE), (1, 0, 2))
    key_value_heads = jnp.transpose(key_value_sequence.reshape(SEQUENCE_LENGTH, KEY_VALUE_HEADS, 2 * HEAD_SIZE), (1, 0, 2))
    owning_head = jnp.arange(QUERY_HEAD_COUNT, dtype=jnp.int32) // query_group
    key_heads = key_value_heads[owning_head][:, :, :HEAD_SIZE]
    value_heads = key_value_heads[owning_head][:, :, HEAD_SIZE:]
    query_part, key_portion, value_portion = lax.map(head_backward, (query_heads, grad_heads, out_heads, key_heads, value_heads))
    key_total_sum = jnp.sum(key_portion.reshape(KEY_VALUE_HEADS, query_group, SEQUENCE_LENGTH, HEAD_SIZE), axis=1)
    value_total_sum = jnp.sum(value_portion.reshape(KEY_VALUE_HEADS, query_group, SEQUENCE_LENGTH, HEAD_SIZE), axis=1)
    query_out = jnp.transpose(query_part, (1, 0, 2)).reshape(SEQUENCE_LENGTH, QUERY_HEAD_COUNT * HEAD_SIZE).astype(jnp.bfloat16)
    key_value_joined = jnp.concatenate([key_total_sum, value_total_sum], axis=-1)
    key_value_output = jnp.transpose(key_value_joined, (1, 0, 2)).reshape(SEQUENCE_LENGTH, KEY_VALUE_HEADS * 2 * HEAD_SIZE).astype(jnp.bfloat16)
    return query_out, key_value_output


def reference(grad_out, routes, gate_probs, saved_pre, down_weight, gate_up_weight, queries, keys_values, attn_grad, attn_out):
    moe_input_grad, prob_grad = moe_backward(grad_out, routes, gate_probs, saved_pre, down_weight, gate_up_weight)
    query_grad, kv_grad = lax.map(sequence_backward, (queries, attn_grad, attn_out, keys_values))
    return moe_input_grad, prob_grad, query_grad, kv_grad
```

```python
import functools

import jax
import jax.numpy as jnp
from jax import lax
from jax.experimental import pallas as pl
from jax.experimental.pallas import tpu as pltpu
from jax.sharding import PartitionSpec as P

HEAD = 128
BF, F32 = jnp.bfloat16, jnp.float32
LOG2E = 1.4426950408889634
VMEM = 48 * 1024 * 1024
GROUPS = ((0, 1, 2), (3,), (4,))


def mm(a, b, dims=((1,), (0,))):
    return lax.dot_general(a, b, (dims, ((), ())), preferred_element_type=F32)


def iota(shape, dim):
    return lax.broadcasted_iota(jnp.int32, shape, dim)


def as_bf(mask):
    return jnp.where(mask, 1.0, 0.0).astype(BF)


def params(**kw):
    return pltpu.CompilerParams(vmem_limit_bytes=VMEM, **kw)


def cost(flops, nbytes, exps=0):
    return pl.CostEstimate(flops=flops, bytes_accessed=nbytes, transcendentals=exps)


def dispatch_kernel(routes_ref, left_ref, right_ref, send_ref, mask_ref, turned):
    @pl.when(pl.program_id(0) == 0)
    def _():
        tok = routes_ref.shape[0]
        route = routes_ref[...]
        lane = iota((tok, tok), 1)
        hot = route == lane
        lower = iota((tok, tok), 0) > lane
        earlier = mm(as_bf(lower), as_bf(hot))
        slot = jnp.sum(jnp.where(hot, earlier, 0.0), axis=1, keepdims=True).astype(jnp.int32)
        first = jnp.where(slot < 8, route * 8 + slot, -1)
        second = jnp.where(slot < 8, -8, route * 8 + slot - 8)
        for i, key in enumerate((first, second, second + 4)):
            one = jnp.where(key == lane, 1.0, 0.0)
            mask_ref[i] = one.astype(BF)
            turned[i] = one.T.astype(BF)

    left, right = left_ref[...], right_ref[...]
    w = left.shape[1]
    send_ref[:, :w] = mm(turned[0], left).astype(BF)
    send_ref[:, w : 2 * w] = mm(turned[0], right).astype(BF)
    send_ref[:, 2 * w :] = (mm(turned[1], left) + mm(turned[2], right)).astype(BF)


def dispatch(routes, grad):
    tok, width = grad.shape
    steps = 4
    w = width // (2 * steps)
    return pl.pallas_call(
        dispatch_kernel,
        grid=(steps,),
        in_specs=[
            pl.BlockSpec((tok, 1), lambda j: (0, 0)),
            pl.BlockSpec((tok, w), lambda j: (0, j)),
            pl.BlockSpec((tok, w), lambda j: (0, j + steps)),
        ],
        out_specs=[
            pl.BlockSpec((tok, 3 * w), lambda j: (0, j)),
            pl.BlockSpec((3, tok, tok), lambda j: (0, 0, 0)),
        ],
        out_shape=[
            jax.ShapeDtypeStruct((tok, 3 * steps * w), BF),
            jax.ShapeDtypeStruct((3, tok, tok), BF),
        ],
        scratch_shapes=[pltpu.VMEM((3, tok, tok), BF)],
        compiler_params=params(dimension_semantics=("arbitrary",)),
        cost_estimate=cost(4 * tok * tok * width, 5 * tok * width),
        name="dispatch",
    )(routes, grad, grad)


def hidden_kernel(rows_ref, dl_ref, dr_ref, pre_ref, grad_ref, prob_ref, acc_l, acc_r):
    j = pl.program_id(0)
    half = rows_ref.shape[0]
    w = dl_ref.shape[1]
    hidden = dl_ref.shape[0]
    extra = rows_ref[:, 2 * w :]
    left = mm(jnp.concatenate([rows_ref[:, :w], extra], 0), dl_ref[...], ((1,), (1,)))
    right = mm(jnp.concatenate([rows_ref[:, w : 2 * w], extra], 0), dr_ref[...], ((1,), (1,)))

    @pl.when(j == 0)
    def _():
        acc_l[...] = left
        acc_r[...] = right

    @pl.when(j > 0)
    def _():
        acc_l[...] += left
        acc_r[...] += right

    @pl.when(j == pl.num_programs(0) - 1)
    def _():
        slots = pre_ref.shape[0]
        row = iota((2 * half, slots), 0)
        inner = row & (half - 1)
        group = inner >> 3
        source = group * 12 + jnp.where(row < half, inner & 7, 8 + (inner & 3))
        pick = as_bf(source == iota((2 * half, slots), 1))
        lane = iota((half, 128), 1)
        probs = jnp.zeros((half, 128), F32)
        for part in range(2):
            here = slice(part * half, (part + 1) * half)
            chosen = pick[here]
            gate = mm(chosen, pre_ref[:, :hidden])
            up = mm(chosen, pre_ref[:, hidden:])
            if part == 0:
                down = acc_l[here] + acc_r[here]
            else:
                low = (iota((half, hidden), 0) & 7) < 4
                mixed = jnp.where(low, acc_l[here], acc_r[here]).reshape(half // 8, 8, hidden)
                down = (mixed + pltpu.roll(mixed, 4, 1)).reshape(half, hidden)
            sigma = jax.nn.sigmoid(gate)
            swish = gate * sigma
            prob = jnp.sum(down * swish * up, axis=1, keepdims=True)
            probs = jnp.where(lane == part, prob, probs)
            grad_ref[here, :hidden] = (
                down * up * sigma * (1.0 + gate * (1.0 - sigma))
            ).astype(BF)
            grad_ref[here, hidden:] = (down * swish).astype(BF)
        prob_ref[...] = probs.astype(BF)


def hidden_grad(rows, down, pre):
    half = rows.shape[0]
    hidden, width = down.shape
    steps = 4
    w = width // (2 * steps)
    return pl.pallas_call(
        hidden_kernel,
        grid=(steps,),
        in_specs=[
            pl.BlockSpec((half, 3 * w), lambda j: (0, j)),
            pl.BlockSpec((hidden, w), lambda j: (0, j)),
            pl.BlockSpec((hidden, w), lambda j: (0, j + steps)),
            pl.BlockSpec(pre.shape, lambda j: (0, 0)),
        ],
        out_specs=[
            pl.BlockSpec((2 * half, 2 * hidden), lambda j: (0, 0)),
            pl.BlockSpec((half, 128), lambda j: (0, 0)),
        ],
        out_shape=[
            jax.ShapeDtypeStruct((2 * half, 2 * hidden), BF),
            jax.ShapeDtypeStruct((half, 128), BF),
        ],
        scratch_shapes=[pltpu.VMEM((2 * half, hidden), F32)] * 2,
        compiler_params=params(dimension_semantics=("arbitrary",)),
        cost_estimate=cost(4 * half * width * hidden, 2 * hidden * width),
        name="hidden_grad",
    )(rows, down, down, pre)


def columns_kernel(sizes, with_prob, *refs):
    grad_ref = refs[0]
    shards = refs[1 : 1 + sum(sizes)]
    out_ref = refs[-1]
    half = grad_ref.shape[0] // 2
    low = (iota((half, 128), 0) & 7) < 4
    at = 0
    for n, size in enumerate(sizes):
        parts = [r[...] for r in shards[at : at + size]]
        at += size
        shard = parts[0] if size == 1 else jnp.concatenate(parts, 0)
        out = mm(grad_ref[...], shard, ((1,), (1,)))
        out_ref[:, n * 384 : n * 384 + 256] = out[:half].astype(BF)
        out_ref[:, n * 384 + 256 : (n + 1) * 384] = jnp.where(
            low, out[half:, :128], out[half:, 128:]
        ).astype(BF)
    if with_prob:
        out_ref[:, len(sizes) * 384 :] = refs[-2][...]


def columns(grad, shards, prob):
    half = grad.shape[0] // 2
    sizes = tuple(len(s) for s in shards)
    flat = [r for s in shards for r in s]
    wide = 384 * len(shards) + (0 if prob is None else 128)
    rest = [] if prob is None else [prob]
    return pl.pallas_call(
        functools.partial(columns_kernel, sizes, prob is not None),
        out_shape=jax.ShapeDtypeStruct((half, wide), BF),
        compiler_params=params(),
        cost_estimate=cost(
            2 * grad.size * 256 * len(shards), 2 * (grad.size + 256 * grad.shape[1] * len(shards))
        ),
        name="columns",
    )(grad, *flat, *rest)


def combine_kernel(counts, ids_ref, mask_ref, gate_ref, *refs):
    arrived, (out_ref, prob_ref) = refs[:-2], refs[-2:]
    first, low, high = mask_ref[0], mask_ref[1], mask_ref[2]
    gate = gate_ref[...]
    place = 0
    for n, (ref, count) in enumerate(zip(arrived, counts)):
        for k in range(count):
            main = ref[:, k * 384 : k * 384 + 256]
            extra = ref[:, k * 384 + 256 : (k + 1) * 384]
            picked = mm(first, main) + jnp.concatenate([mm(low, extra), mm(high, extra)], 1)
            where = pl.multiple_of(ids_ref[place] * 256, 256)
            out_ref[:, pl.ds(where, 256)] = (gate * picked).astype(BF)
            place += 1
        if n == 0:
            probs = ref[:, count * 384 :]
            prob_ref[...] = (mm(first, probs)[:, :1] + mm(low, probs)[:, 1:2]).astype(BF)


def combine(ids, masks, gate, arrived, counts, width):
    tok = gate.shape[0]
    vmem = pl.BlockSpec(memory_space=pltpu.VMEM)
    return pl.pallas_call(
        functools.partial(combine_kernel, counts),
        in_specs=[pl.BlockSpec(memory_space=pltpu.SMEM)] + [vmem] * (2 + len(arrived)),
        out_specs=[vmem, vmem],
        out_shape=[
            jax.ShapeDtypeStruct((tok, width), BF),
            jax.ShapeDtypeStruct((tok, 1), BF),
        ],
        compiler_params=params(),
        cost_estimate=cost(4 * tok * tok * width, 6 * tok * width),
        name="combine",
    )(ids, masks, gate, *arrived)


def delta_kernel(grad_ref, out_ref, delta_ref):
    heads = delta_ref.shape[0]
    for h in range(heads):
        cols = slice(h * HEAD, (h + 1) * HEAD)
        product = grad_ref[:, cols].astype(F32) * out_ref[:, cols].astype(F32)
        delta_ref[h : h + 1, :] = jnp.sum(product.T, axis=0, keepdims=True)


def deltas(grad, out):
    tok, width = grad.shape
    return pl.pallas_call(
        delta_kernel,
        out_shape=jax.ShapeDtypeStruct((width // HEAD, tok), F32),
        compiler_params=params(),
        cost_estimate=cost(2 * tok * width, 4 * tok * width),
        name="deltas",
    )(grad, out)


def attend_kernel(
    place_ref, q_ref, g_ref, qo_ref, go_ref, d_ref, do_ref, *refs
):
    kv = refs[:8]
    dq_ref, dqo_ref, dkv_ref, turned, kept = refs[8:]
    h = pl.program_id(0)
    heads = pl.num_programs(0)
    chip, core = place_ref[0], place_ref[1]
    tok = q_ref.shape[0]
    rows = 2 * tok
    scale = HEAD**-0.5

    @pl.when(h == 0)
    def _():
        dkv_ref[...] = jnp.zeros_like(dkv_ref)
        for s in range(8):
            turned[s] = kv[s][:, :HEAD].T

    query = jnp.concatenate([q_ref[...], qo_ref[...]], 0)
    grad = jnp.concatenate([g_ref[...], go_ref[...]], 0)
    delta = jnp.concatenate(
        [d_ref[pl.ds(core * heads + h, 1), :], do_ref[pl.ds(h, 1), :]], 1
    )
    valid = [None] + [chip >= s for s in range(1, 5)] + [chip + s >= 8 for s in range(1, 4)]
    source = [lax.rem(chip + 8 - s, 8) for s in range(5)] + [
        lax.rem(chip + s, 8) for s in range(1, 4)
    ]
    flip = core * tok
    key_pos = iota((rows, rows), 0) ^ flip
    row_pos = iota((rows, rows), 1) ^ flip
    highest = None
    for s in range(8):
        scores = mm(kv[s][:, :HEAD], query, ((1,), (1,)))
        if s == 0:
            scores = jnp.where(key_pos <= row_pos, scores, -1e30)
        kept[s] = scores
        top = jnp.max(scores, axis=0, keepdims=True)
        if s == 0:
            highest = top
        else:
            highest = jnp.maximum(highest, jnp.where(valid[s], top, -1e30))
    total = jnp.zeros((1, rows), F32)
    for s in range(8):
        base = highest if s == 0 else jnp.where(valid[s], highest, 1e30)
        expo = jnp.exp2((kept[s] - base) * (scale * LOG2E))
        kept[s] = expo
        total = total + jnp.sum(expo, axis=0, keepdims=True)
    share = 1.0 / total
    dq = jnp.zeros((HEAD, rows), F32)
    for s in range(8):
        probs = kept[s] * share
        part = mm(kv[s][:, HEAD:], grad, ((1,), (1,)))
        score_grad = (probs * (part - delta)).astype(BF)
        at = pl.ds(pl.multiple_of(source[s] * rows, rows), rows)
        dkv_ref[at, HEAD:] += mm(probs.astype(BF), grad)
        dkv_ref[at, :HEAD] += mm(score_grad, query)
        dq = dq + mm(turned[s], score_grad)
    dq = (dq * scale).T.astype(BF)
    dq_ref[...] = dq[:tok]
    dqo_ref[...] = dq[tok:]


def attend(place, queries, grads, others, delta, delta_other, kv):
    tok, width = queries.shape
    heads = width // HEAD // 2
    head = (tok, HEAD)
    rows = 2 * tok
    whole = lambda a: pl.BlockSpec(a.shape, lambda h, p: (0,) * a.ndim)
    return pl.pallas_call(
        attend_kernel,
        grid_spec=pltpu.PrefetchScalarGridSpec(
            num_scalar_prefetch=1,
            grid=(heads,),
            in_specs=[
                pl.BlockSpec(head, lambda h, p: (0, p[1] * heads + h)),
                pl.BlockSpec(head, lambda h, p: (0, p[1] * heads + h)),
                pl.BlockSpec(head, lambda h, p: (0, h)),
                pl.BlockSpec(head, lambda h, p: (0, heads + h)),
                whole(delta),
                whole(delta_other),
            ]
            + [whole(a) for a in kv],
            out_specs=[
                pl.BlockSpec(head, lambda h, p: (0, h)),
                pl.BlockSpec(head, lambda h, p: (0, h)),
                pl.BlockSpec((8 * rows, 2 * HEAD), lambda h, p: (0, 0)),
            ],
            scratch_shapes=[
                pltpu.VMEM((8, HEAD, rows), BF),
                pltpu.VMEM((8, rows, rows), F32),
            ],
        ),
        out_shape=[
            jax.ShapeDtypeStruct((tok, width // 2), BF),
            jax.ShapeDtypeStruct((tok, width // 2), BF),
            jax.ShapeDtypeStruct((8 * rows, 2 * HEAD), F32),
        ],
        compiler_params=params(dimension_semantics=("arbitrary",)),
        cost_estimate=cost(
            20 * heads * 8 * rows * rows * HEAD, 12 * tok * width, heads * 8 * rows * rows
        ),
        name="attend",
    )(place, queries, grads, others, others, delta, delta_other, *kv)


def along(x, step):
    return lax.ppermute(x, "ctx", [(i, (i + 2 * step) % 16) for i in range(16)])


def swap(x):
    return lax.ppermute(x, "ctx", [(i, i ^ 1) for i in range(16)])


def exchange(x):
    groups = lax.axis_size("exp")
    cut = x.reshape(groups, x.shape[0] // groups, x.shape[1])
    out = lax.all_to_all(cut, "exp", split_axis=0, concat_axis=0, tiled=True)
    return out.reshape(x.shape)


def body(
    grad_out,
    routes,
    gate_probs,
    saved_pre,
    down_weight,
    gate_up_weight,
    queries,
    keys_values,
    attn_grad,
    attn_out,
):
    width = grad_out.shape[2]
    index = lax.axis_index("ctx")
    chip, core = index // 2, index % 2
    place = jnp.stack([chip, core]).astype(jnp.int32)
    query, grad, kv_rows = queries[0], attn_grad[0], keys_values[0]
    half = width // 2

    def mine(x, n):
        return lax.dynamic_slice_in_dim(x, core * n, n, 1)

    def theirs(x, n):
        return lax.dynamic_slice_in_dim(x, (1 - core) * n, n, 1)

    own = jnp.concatenate([mine(kv_rows, 2 * HEAD), swap(theirs(kv_rows, 2 * HEAD))], 0)
    up, down = [own], [own]
    for s in range(4):
        up.append(along(up[-1], 1))
        if s < 3:
            down.append(along(down[-1], -1))
    kv = up + down[1:]

    full_down = lax.all_gather(down_weight[0], "ctx", axis=1, tiled=True)
    shard = gate_up_weight[0]
    fore, back = [shard], [shard]
    for s in range(3):
        fore.append(along(fore[-1], 1))
        back.append(along(back[-1], -1))
    mid = shard.shape[0] // 2
    last = (along(fore[3][:mid], 1), along(back[3][mid:], -1))
    steps = [[((shard,), chip, core), ((swap(shard),), chip, 1 - core)]]
    for s in range(1, 4):
        steps.append(
            [
                ((fore[s],), chip - s, core),
                ((back[s],), chip + s, core),
                ((swap(fore[s]),), chip - s, 1 - core),
                ((swap(back[s]),), chip + s, 1 - core),
            ]
        )
    steps.append(
        [(last, chip + 4, core), (tuple(swap(x) for x in last), chip + 4, 1 - core)]
    )

    send, masks = dispatch(routes[0], grad_out[0])
    arrived = exchange(send)

    delta = deltas(grad, attn_out[0])
    others = swap(jnp.concatenate([theirs(query, half), theirs(grad, half)], 1))
    n_heads = delta.shape[0] // 2
    delta_other = swap(lax.dynamic_slice_in_dim(delta, (1 - core) * n_heads, n_heads, 0))
    dq_own, dq_other, dkv = attend(place, query, grad, others, delta, delta_other, kv)
    dq_back = swap(dq_other)
    query_grad = jnp.where(
        core == 0,
        jnp.concatenate([dq_own, dq_back], 1),
        jnp.concatenate([dq_back, dq_own], 1),
    )
    chips = [[2 * z + c for z in range(8)] for c in range(2)]
    summed = lax.psum_scatter(
        dkv, "ctx", scatter_dimension=0, tiled=True, axis_index_groups=chips
    )
    factor = jnp.where(jnp.arange(2 * HEAD) < HEAD, F32(HEAD**-0.5), F32(1.0))
    summed = (summed * factor).astype(BF)
    tok = kv_rows.shape[0]
    kv_own, kv_back = summed[:tok], swap(summed[tok:])
    kv_grad = jnp.where(
        core == 0,
        jnp.concatenate([kv_own, kv_back], 1),
        jnp.concatenate([kv_back, kv_own], 1),
    )

    hidden, prob = hidden_grad(arrived, full_down, saved_pre[0, 0])
    back_rows, counts, ids = [], [], []
    for n, group in enumerate(GROUPS):
        members = [m for s in group for m in steps[s]]
        out = columns(hidden, [m[0] for m in members], prob if n == 0 else None)
        back_rows.append(exchange(out))
        counts.append(len(members))
        ids += [((m[1] + 8) % 8) * 2 + m[2] for m in members]
    moe_grad, prob_grad = combine(
        jnp.stack(ids).astype(jnp.int32),
        masks,
        gate_probs[0],
        back_rows,
        tuple(counts),
        width,
    )
    return moe_grad[None], prob_grad[None], query_grad[None], kv_grad[None]


def solution(mesh):
    tokens = P("exp", "ctx", None)
    placed = (
        tokens,
        tokens,
        tokens,
        P("ctx", "exp", None, None),
        P("exp", None, "ctx"),
        tokens,
        tokens,
        tokens,
        tokens,
        tokens,
    )
    return jax.shard_map(
        body,
        mesh=mesh,
        in_specs=placed,
        out_specs=(tokens, tokens, tokens, tokens),
        check_vma=False,
    )
```

```python
import functools

import jax
import jax.numpy as jnp
from jax import lax
from jax.experimental import pallas as pl
from jax.experimental.pallas import tpu as pltpu
from jax.sharding import PartitionSpec as P

HEAD = 128
BF, F32 = jnp.bfloat16, jnp.float32
LOG2E = 1.4426950408889634
VMEM = 48 * 1024 * 1024
GROUPS = ((0, 1, 2), (3, 4))
PARTS = (4, 4, 4, 4)
HOLD = {2: 1}


def mm(a, b, dims=((1,), (0,))):
    return lax.dot_general(a, b, (dims, ((), ())), preferred_element_type=F32)


def iota(shape, dim):
    return lax.broadcasted_iota(jnp.int32, shape, dim)


def as_bf(mask):
    return jnp.where(mask, 1.0, 0.0).astype(BF)


def params(**kw):
    return pltpu.CompilerParams(vmem_limit_bytes=VMEM, **kw)


def cost(flops, nbytes, exps=0):
    return pl.CostEstimate(flops=flops, bytes_accessed=nbytes, transcendentals=exps)


def dispatch_kernel(routes_ref, left_ref, right_ref, send_ref, mask_ref, turned):
    @pl.when(pl.program_id(0) == 0)
    def _():
        tok = routes_ref.shape[0]
        route = routes_ref[...]
        lane = iota((tok, tok), 1)
        hot = route == lane
        lower = iota((tok, tok), 0) > lane
        earlier = mm(as_bf(lower), as_bf(hot))
        slot = jnp.sum(jnp.where(hot, earlier, 0.0), axis=1, keepdims=True).astype(jnp.int32)
        first = jnp.where(slot < 8, route * 8 + slot, -1)
        second = jnp.where(slot < 8, -8, route * 8 + slot - 8)
        for i, key in enumerate((first, second, second + 4)):
            one = jnp.where(key == lane, 1.0, 0.0)
            mask_ref[i] = one.astype(BF)
            turned[i] = one.T.astype(BF)

    left, right = left_ref[...], right_ref[...]
    w = left.shape[1]
    send_ref[:, :w] = mm(turned[0], left).astype(BF)
    send_ref[:, w : 2 * w] = mm(turned[0], right).astype(BF)
    send_ref[:, 2 * w :] = (mm(turned[1], left) + mm(turned[2], right)).astype(BF)


def dispatch(routes, grad):
    tok, width = grad.shape
    steps = 4
    w = width // (2 * steps)
    return pl.pallas_call(
        dispatch_kernel,
        grid=(steps,),
        in_specs=[
            pl.BlockSpec((tok, 1), lambda j: (0, 0)),
            pl.BlockSpec((tok, w), lambda j: (0, j)),
            pl.BlockSpec((tok, w), lambda j: (0, j + steps)),
        ],
        out_specs=[
            pl.BlockSpec((tok, 3 * w), lambda j: (0, j)),
            pl.BlockSpec((3, tok, tok), lambda j: (0, 0, 0)),
        ],
        out_shape=[
            jax.ShapeDtypeStruct((tok, 3 * steps * w), BF),
            jax.ShapeDtypeStruct((3, tok, tok), BF),
        ],
        scratch_shapes=[pltpu.VMEM((3, tok, tok), BF)],
        compiler_params=params(dimension_semantics=("arbitrary",)),
        cost_estimate=cost(4 * tok * tok * width, 5 * tok * width),
        name="dispatch",
    )(routes, grad, grad)


def hidden_kernel(rows_ref, dl_ref, dr_ref, pre_ref, grad_ref, prob_ref, acc_l, acc_r):
    j = pl.program_id(0)
    half = rows_ref.shape[0]
    w = dl_ref.shape[1]
    hidden = dl_ref.shape[0]
    extra = rows_ref[:, 2 * w :]
    left = mm(jnp.concatenate([rows_ref[:, :w], extra], 0), dl_ref[...], ((1,), (1,)))
    right = mm(jnp.concatenate([rows_ref[:, w : 2 * w], extra], 0), dr_ref[...], ((1,), (1,)))

    @pl.when(j == 0)
    def _():
        acc_l[...] = left
        acc_r[...] = right

    @pl.when(j > 0)
    def _():
        acc_l[...] += left
        acc_r[...] += right

    @pl.when(j == pl.num_programs(0) - 1)
    def _():
        slots = pre_ref.shape[0]
        row = iota((2 * half, slots), 0)
        inner = row & (half - 1)
        group = inner >> 3
        source = group * 12 + jnp.where(row < half, inner & 7, 8 + (inner & 3))
        pick = as_bf(source == iota((2 * half, slots), 1))
        lane = iota((half, 128), 1)
        probs = jnp.zeros((half, 128), F32)
        for part in range(2):
            here = slice(part * half, (part + 1) * half)
            chosen = pick[here]
            gate = mm(chosen, pre_ref[:, :hidden])
            up = mm(chosen, pre_ref[:, hidden:])
            if part == 0:
                down = acc_l[here] + acc_r[here]
            else:
                low = (iota((half, hidden), 0) & 7) < 4
                mixed = jnp.where(low, acc_l[here], acc_r[here]).reshape(half // 8, 8, hidden)
                down = (mixed + pltpu.roll(mixed, 4, 1)).reshape(half, hidden)
            sigma = jax.nn.sigmoid(gate)
            swish = gate * sigma
            prob = jnp.sum(down * swish * up, axis=1, keepdims=True)
            probs = jnp.where(lane == part, prob, probs)
            grad_ref[here, :hidden] = (
                down * up * sigma * (1.0 + gate * (1.0 - sigma))
            ).astype(BF)
            grad_ref[here, hidden:] = (down * swish).astype(BF)
        prob_ref[...] = probs.astype(BF)


def hidden_grad(rows, down, pre):
    half = rows.shape[0]
    hidden, width = down.shape
    steps = 4
    w = width // (2 * steps)
    return pl.pallas_call(
        hidden_kernel,
        grid=(steps,),
        in_specs=[
            pl.BlockSpec((half, 3 * w), lambda j: (0, j)),
            pl.BlockSpec((hidden, w), lambda j: (0, j)),
            pl.BlockSpec((hidden, w), lambda j: (0, j + steps)),
            pl.BlockSpec(pre.shape, lambda j: (0, 0)),
        ],
        out_specs=[
            pl.BlockSpec((2 * half, 2 * hidden), lambda j: (0, 0)),
            pl.BlockSpec((half, 128), lambda j: (0, 0)),
        ],
        out_shape=[
            jax.ShapeDtypeStruct((2 * half, 2 * hidden), BF),
            jax.ShapeDtypeStruct((half, 128), BF),
        ],
        scratch_shapes=[pltpu.VMEM((2 * half, hidden), F32)] * 2,
        compiler_params=params(dimension_semantics=("arbitrary",)),
        cost_estimate=cost(4 * half * width * hidden, 2 * hidden * width),
        name="hidden_grad",
    )(rows, down, down, pre)


def columns_kernel(sizes, with_prob, *refs):
    grad_ref = refs[0]
    shards = refs[1 : 1 + sum(sizes)]
    out_ref = refs[-1]
    half = grad_ref.shape[0] // 2
    low = (iota((half, 128), 0) & 7) < 4
    at = 0
    for n, size in enumerate(sizes):
        parts = [r[...] for r in shards[at : at + size]]
        at += size
        shard = parts[0] if size == 1 else jnp.concatenate(parts, 0)
        out = mm(grad_ref[...], shard, ((1,), (1,)))
        out_ref[:, n * 384 : n * 384 + 256] = out[:half].astype(BF)
        out_ref[:, n * 384 + 256 : (n + 1) * 384] = jnp.where(
            low, out[half:, :128], out[half:, 128:]
        ).astype(BF)
    if with_prob:
        out_ref[:, len(sizes) * 384 :] = refs[-2][...]


def columns(grad, shards, prob):
    half = grad.shape[0] // 2
    sizes = tuple(len(s) for s in shards)
    flat = [r for s in shards for r in s]
    wide = 384 * len(shards) + (0 if prob is None else 128)
    rest = [] if prob is None else [prob]
    return pl.pallas_call(
        functools.partial(columns_kernel, sizes, prob is not None),
        out_shape=jax.ShapeDtypeStruct((half, wide), BF),
        compiler_params=params(),
        cost_estimate=cost(
            2 * grad.size * 256 * len(shards), 2 * (grad.size + 256 * grad.shape[1] * len(shards))
        ),
        name="columns",
    )(grad, *flat, *rest)


def combine_kernel(counts, first, ids_ref, mask_ref, gate_ref, *refs):
    if first:
        arrived, (out_ref, prob_ref) = refs[:-2], refs[-2:]
    else:
        before, arrived, out_ref = refs[0], refs[1:-1], refs[-1]
        out_ref[...] = before[...]
    main_mask, low, high = mask_ref[0], mask_ref[1], mask_ref[2]
    gate = gate_ref[...]
    place = 0
    for ref, count in zip(arrived, counts):
        for k in range(count):
            main = ref[:, k * 384 : k * 384 + 256]
            extra = ref[:, k * 384 + 256 : (k + 1) * 384]
            picked = mm(main_mask, main) + jnp.concatenate([mm(low, extra), mm(high, extra)], 1)
            where = pl.multiple_of(ids_ref[place] * 256, 256)
            out_ref[:, pl.ds(where, 256)] = (gate * picked).astype(BF)
            place += 1
    if first:
        probs = arrived[0][:, counts[0] * 384 :]
        prob_ref[...] = (mm(main_mask, probs)[:, :1] + mm(low, probs)[:, 1:2]).astype(BF)


def combine(ids, masks, gate, before, arrived, counts, width):
    tok = gate.shape[0]
    first = before is None
    vmem = pl.BlockSpec(memory_space=pltpu.VMEM)
    operands = ([] if first else [before]) + list(arrived)
    out_shape = [jax.ShapeDtypeStruct((tok, width), BF)]
    if first:
        out_shape.append(jax.ShapeDtypeStruct((tok, 1), BF))
    return pl.pallas_call(
        functools.partial(combine_kernel, counts, first),
        in_specs=[pl.BlockSpec(memory_space=pltpu.SMEM)] + [vmem] * (2 + len(operands)),
        out_specs=[vmem] * len(out_shape),
        out_shape=out_shape,
        compiler_params=params(),
        cost_estimate=cost(4 * tok * tok * 256 * sum(counts), 6 * tok * width),
        name="combine",
    )(ids, masks, gate, *operands)


def delta_kernel(grad_ref, out_ref, delta_ref):
    heads = delta_ref.shape[0]
    for h in range(heads):
        cols = slice(h * HEAD, (h + 1) * HEAD)
        product = grad_ref[:, cols].astype(F32) * out_ref[:, cols].astype(F32)
        delta_ref[h : h + 1, :] = jnp.sum(product.T, axis=0, keepdims=True)


def deltas(grad, out):
    tok, width = grad.shape
    return pl.pallas_call(
        delta_kernel,
        out_shape=jax.ShapeDtypeStruct((width // HEAD, tok), F32),
        compiler_params=params(),
        cost_estimate=cost(2 * tok * width, 4 * tok * width),
        name="deltas",
    )(grad, out)


def attend_kernel(first, last, pairs, start, place_ref, *refs):
    q_ref, g_ref, qo_ref, go_ref, d_ref, do_ref = refs[:6]
    kv = refs[6:14]
    at = 14
    if not first:
        turned, before = refs[at : at + 2]
        at += 4
    dq_ref, dqo_ref = refs[at : at + 2]
    at += 2
    if first:
        turned = refs[at]
        at += 1
    if last:
        sent_ref = refs[at]
        at += 1
    sums, kept, low_probs, low_grads = refs[at : at + 4]
    i = pl.program_id(0)
    chip, core = place_ref[0], place_ref[1]
    tok = q_ref.shape[0]
    block = 2 * tok
    rows = 2 * block
    scale = HEAD**-0.5
    factor = scale * LOG2E
    n_heads = do_ref.shape[0]
    valid = [None] + [chip >= s for s in range(1, 5)] + [chip + s >= 8 for s in range(1, 4)]

    @pl.when(i == 0)
    def _():
        if first:
            sums[...] = jnp.zeros_like(sums)
            for s in range(8):
                turned[:, s * block : (s + 1) * block] = kv[s][:, :HEAD].T
        else:
            sums[...] = before[...]

    def stack(own, other):
        return jnp.concatenate(
            [own[:, :HEAD], other[:, :HEAD], own[:, HEAD:], other[:, HEAD:]], 0
        )

    query = stack(q_ref, qo_ref)
    grad = stack(g_ref, go_ref)
    head = start + 2 * i
    delta = jnp.concatenate(
        [
            r[pl.ds(at_head, 1), :]
            for n in range(2)
            for r, at_head in ((d_ref, core * n_heads + head + n), (do_ref, head + n))
        ],
        1,
    )
    highest = total = None
    bases = []
    for s in range(8):
        here = slice(s * block, (s + 1) * block)
        scores = mm(kv[s][:, :HEAD], query, ((1,), (1,)))
        if s == 0:
            flip = core * tok
            key_pos = iota((block, rows), 0) ^ flip
            row_pos = (iota((block, rows), 1) & (block - 1)) ^ flip
            scores = jnp.where(key_pos <= row_pos, scores, -1e30)
        top = jnp.max(scores, axis=0, keepdims=True)
        if s == 0:
            new = base = top
        else:
            new = jnp.maximum(highest, jnp.where(valid[s], top, -1e30))
            base = jnp.where(valid[s], new, 1e30)
        expo = jnp.exp2((scores - base) * factor)
        kept[here, :] = expo
        fresh = jnp.sum(expo, axis=0, keepdims=True)
        total = fresh if s == 0 else total * jnp.exp2((highest - new) * factor) + fresh
        highest = new
        bases.append(new)
    inverse = 1.0 / total
    for s in range(8):
        here = slice(s * block, (s + 1) * block)
        share = inverse * jnp.exp2((bases[s] - highest) * factor)
        probs = kept[here, :] * share
        part = mm(kv[s][:, HEAD:], grad, ((1,), (1,)))
        low_grads[here, :] = (probs * (part - delta)).astype(BF)
        low_probs[here, :] = probs.astype(BF)
    sums[:, HEAD:] += mm(low_probs[...], grad)
    sums[:, :HEAD] += mm(low_grads[...], query)
    dq = (mm(turned[...], low_grads[...]) * scale).T.astype(BF)
    for n in range(2):
        cols = slice(n * HEAD, (n + 1) * HEAD)
        dq_ref[:, cols] = dq[n * block : n * block + tok]
        dqo_ref[:, cols] = dq[n * block + tok : (n + 1) * block]

    if last:

        @pl.when(i == pairs - 1)
        def _():
            for s in range(8):
                source = lax.rem(chip + (8 - s if s < 5 else s - 4), 8)
                to = pl.ds(pl.multiple_of(source * block, block), block)
                sent_ref[to, :] = sums[s * block : (s + 1) * block, :]


def attend(first, last, start, heads, place, queries, grads, others, delta, delta_other, kv, carry):
    tok, width = queries.shape
    n_heads = width // HEAD // 2
    pairs = heads // 2
    pair = (tok, 2 * HEAD)
    block, rows = 2 * tok, 4 * tok
    lead = start // 2

    def whole(a):
        return pl.BlockSpec(a.shape, lambda i, p: (0,) * len(a.shape))

    half_pairs = n_heads // 2
    sums = jax.ShapeDtypeStruct((8 * block, 2 * HEAD), F32)
    turned = jax.ShapeDtypeStruct((HEAD, 8 * block), BF)
    out_shape = [
        jax.ShapeDtypeStruct((tok, width), BF),
        jax.ShapeDtypeStruct((tok, width // 2), BF),
    ]
    out_specs = [
        pl.BlockSpec(pair, lambda i, p: (0, p[1] * half_pairs + lead + i)),
        pl.BlockSpec(pair, lambda i, p: (0, lead + i)),
    ]
    scratch = [
        pltpu.VMEM((8 * block, rows), F32),
        pltpu.VMEM((8 * block, rows), BF),
        pltpu.VMEM((8 * block, rows), BF),
    ]
    extra = []
    if first:
        extra.append(turned)
    if last:
        extra.append(sums)
        scratch = [pltpu.VMEM(sums.shape, F32)] + scratch
    else:
        extra.append(sums)
    mine = pl.BlockSpec(pair, lambda i, p: (0, p[1] * half_pairs + lead + i))
    in_specs = [
        mine,
        mine,
        pl.BlockSpec(pair, lambda i, p: (0, lead + i)),
        pl.BlockSpec(pair, lambda i, p: (0, half_pairs + lead + i)),
        whole(delta),
        whole(delta_other),
    ]
    in_specs += [whole(a) for a in kv]
    more = list(kv)
    alias = {}
    if not first:
        in_specs += [whole(a) for a in carry[:2]] + [pl.BlockSpec(memory_space=pl.ANY)] * 2
        more += list(carry)
        alias = {17: 0, 18: 1}
    return pl.pallas_call(
        functools.partial(attend_kernel, first, last, pairs, start),
        grid_spec=pltpu.PrefetchScalarGridSpec(
            num_scalar_prefetch=1,
            grid=(pairs,),
            in_specs=in_specs,
            out_specs=out_specs + [whole(a) for a in extra],
            scratch_shapes=scratch,
        ),
        out_shape=out_shape + extra,
        input_output_aliases=alias,
        compiler_params=params(dimension_semantics=("arbitrary",)),
        cost_estimate=cost(
            40 * heads * 8 * block * block * HEAD, 12 * tok * width, heads * 8 * block * block
        ),
        name="attend",
    )(place, queries, grads, others, others, delta, delta_other, *more)


def hold(x, until):
    return lax.optimization_barrier((x, until))[0]


def along(x, step):
    return lax.ppermute(x, "ctx", [(i, (i + 2 * step) % 16) for i in range(16)])


def swap(x):
    return lax.ppermute(x, "ctx", [(i, i ^ 1) for i in range(16)])


def exchange(x):
    groups = lax.axis_size("exp")
    cut = x.reshape(groups, x.shape[0] // groups, x.shape[1])
    out = lax.all_to_all(cut, "exp", split_axis=0, concat_axis=0, tiled=True)
    return out.reshape(x.shape)


def body(
    grad_out,
    routes,
    gate_probs,
    saved_pre,
    down_weight,
    gate_up_weight,
    queries,
    keys_values,
    attn_grad,
    attn_out,
):
    width = grad_out.shape[2]
    index = lax.axis_index("ctx")
    chip, core = index // 2, index % 2
    place = jnp.stack([chip, core]).astype(jnp.int32)
    query, grad, kv_rows = queries[0], attn_grad[0], keys_values[0]
    half = width // 2

    def mine(x, n):
        return lax.dynamic_slice_in_dim(x, core * n, n, 1)

    def theirs(x, n):
        return lax.dynamic_slice_in_dim(x, (1 - core) * n, n, 1)

    own = jnp.concatenate([mine(kv_rows, 2 * HEAD), swap(theirs(kv_rows, 2 * HEAD))], 0)
    up, down = [own], [own]
    for s in range(4):
        up.append(along(up[-1], 1))
        if s < 3:
            down.append(along(down[-1], -1))
    kv = up + down[1:]

    send, masks = dispatch(routes[0], grad_out[0])
    arrived = exchange(send)

    full_down = lax.all_gather(down_weight[0], "ctx", axis=1, tiled=True)
    shard = gate_up_weight[0]
    begin = hold(shard, (up[3], down[3]))
    fore, back = [begin], [begin]
    for s in range(3):
        fore.append(along(fore[-1], 1))
        back.append(along(back[-1], -1))
    mid = shard.shape[0] // 2
    last = (along(fore[3][:mid], 1), along(back[3][mid:], -1))
    steps = [[((shard,), chip, core), ((swap(shard),), chip, 1 - core)]]
    for s in range(1, 4):
        steps.append(
            [
                ((fore[s],), chip - s, core),
                ((back[s],), chip + s, core),
                ((swap(fore[s]),), chip - s, 1 - core),
                ((swap(back[s]),), chip + s, 1 - core),
            ]
        )
    steps.append(
        [(last, chip + 4, core), (tuple(swap(x) for x in last), chip + 4, 1 - core)]
    )

    delta = deltas(grad, attn_out[0])
    query_late, grad_late = hold((query, grad), up[0])
    others = swap(jnp.concatenate([theirs(query_late, half), theirs(grad_late, half)], 1))
    n_heads = delta.shape[0] // 2
    delta_other = swap(lax.dynamic_slice_in_dim(delta, (1 - core) * n_heads, n_heads, 0))
    carry = None
    for n, heads in enumerate(PARTS):
        begun, ended = n == 0, n == len(PARTS) - 1
        operands = (query, grad, others, delta, delta_other)
        if n == 0:
            operands = hold(operands, send)
        if ended:
            operands = hold(operands, arrived)
        if n in HOLD:
            operands = hold(operands, (fore[HOLD[n]], back[HOLD[n]]))
        outs = attend(begun, ended, sum(PARTS[:n]), heads, place, *operands, kv, carry)
        if begun:
            turned = outs[2]
        carry = (turned, outs[-1], outs[0], outs[1])
    query_grad, dq_other = outs[:2]
    terms = outs[-1]
    dq_back = swap(dq_other)
    chips = [[2 * z + c for z in range(8)] for c in range(2)]
    kv_sum = lax.psum_scatter(
        hold(terms, (fore[3], back[3])), "ctx", scatter_dimension=0, tiled=True, axis_index_groups=chips
    )

    arrived = hold(arrived, terms)
    hidden, prob = hidden_grad(arrived, full_down, saved_pre[0, 0])
    back_rows, counts, ids = [], [], []
    for n, group in enumerate(GROUPS):
        members = [m for s in group for m in steps[s]]
        source = hidden
        if n == 0:
            source = hold(hidden, (fore[3], back[3]))
        if n == 1:
            source = hold(hidden, out)
        out = columns(source, [m[0] for m in members], prob if n == 0 else None)
        if n == 0:
            out = hold(out, last)
        back_rows.append(exchange(out))
        counts.append(len(members))
        ids.append(
            jnp.stack([((m[1] + 8) % 8) * 2 + m[2] for m in members]).astype(jnp.int32)
        )
    moe_grad, prob_grad = combine(
        jnp.concatenate(ids[:-1]), masks, gate_probs[0], None, back_rows[:-1], tuple(counts[:-1]), width
    )
    (moe_grad,) = combine(
        ids[-1], masks, gate_probs[0], moe_grad, back_rows[-1:], tuple(counts[-1:]), width
    )

    kv_sum, dq_back = hold((kv_sum, dq_back), prob_grad)
    query_grad = lax.dynamic_update_slice(query_grad, dq_back, (0, (1 - core) * half))
    factor = jnp.where(jnp.arange(2 * HEAD) < HEAD, F32(HEAD**-0.5), F32(1.0))
    summed = (kv_sum.astype(F32) * factor).astype(BF)
    tok = kv_rows.shape[0]
    kv_own, kv_back = summed[:tok], swap(summed[tok:])
    kv_grad = jnp.where(
        core == 0,
        jnp.concatenate([kv_own, kv_back], 1),
        jnp.concatenate([kv_back, kv_own], 1),
    )
    return moe_grad[None], prob_grad[None], query_grad[None], kv_grad[None]


def solution(mesh):
    tokens = P("exp", "ctx", None)
    placed = (
        tokens,
        tokens,
        tokens,
        P("ctx", "exp", None, None),
        P("exp", None, "ctx"),
        tokens,
        tokens,
        tokens,
        tokens,
        tokens,
    )
    return jax.shard_map(
        body,
        mesh=mesh,
        in_specs=placed,
        out_specs=(tokens, tokens, tokens, tokens),
        check_vma=False,
    )
```

```python
import functools

import jax
import jax.numpy as jnp
from jax import lax
from jax.experimental import pallas as pl
from jax.experimental.pallas import tpu as pltpu
from jax.sharding import PartitionSpec as P

HEAD = 128
BF, F32 = jnp.bfloat16, jnp.float32
LOG2E = 1.4426950408889634
GROUPS = ((0, 1, 2), (3, 4))
PARTS = (4, 4, 4, 4)
HOLD = {2: 1}


def mm(a, b, dims=((1,), (0,))):
    return lax.dot_general(a, b, (dims, ((), ())), preferred_element_type=F32)


def iota(shape, dim):
    return lax.broadcasted_iota(jnp.int32, shape, dim)


def as_bf(mask):
    return jnp.where(mask, 1.0, 0.0).astype(BF)


def params(mib=48, **kw):
    return pltpu.CompilerParams(vmem_limit_bytes=mib * 1024 * 1024, **kw)


def cost(flops, nbytes, exps=0):
    return pl.CostEstimate(flops=flops, bytes_accessed=nbytes, transcendentals=exps)


def dispatch_kernel(routes_ref, left_ref, right_ref, send_ref, mask_ref, turned):
    @pl.when(pl.program_id(0) == 0)
    def _():
        tok = routes_ref.shape[0]
        route = routes_ref[...]
        lane = iota((tok, tok), 1)
        hot = route == lane
        lower = iota((tok, tok), 0) > lane
        earlier = mm(as_bf(lower), as_bf(hot))
        slot = jnp.sum(jnp.where(hot, earlier, 0.0), axis=1, keepdims=True).astype(jnp.int32)
        first = jnp.where(slot < 8, route * 8 + slot, -1)
        second = jnp.where(slot < 8, -8, route * 8 + slot - 8)
        for i, key in enumerate((first, second, second + 4)):
            one = jnp.where(key == lane, 1.0, 0.0)
            mask_ref[i] = one.astype(BF)
            turned[i] = one.T.astype(BF)

    left, right = left_ref[...], right_ref[...]
    w = left.shape[1]
    send_ref[:, :w] = mm(turned[0], left).astype(BF)
    send_ref[:, w : 2 * w] = mm(turned[0], right).astype(BF)
    send_ref[:, 2 * w :] = (mm(turned[1], left) + mm(turned[2], right)).astype(BF)


def dispatch(routes, grad):
    tok, width = grad.shape
    steps = 4
    w = width // (2 * steps)
    return pl.pallas_call(
        dispatch_kernel,
        grid=(steps,),
        in_specs=[
            pl.BlockSpec((tok, 1), lambda j: (0, 0)),
            pl.BlockSpec((tok, w), lambda j: (0, j)),
            pl.BlockSpec((tok, w), lambda j: (0, j + steps)),
        ],
        out_specs=[
            pl.BlockSpec((tok, 3 * w), lambda j: (0, j)),
            pl.BlockSpec((3, tok, tok), lambda j: (0, 0, 0)),
        ],
        out_shape=[
            jax.ShapeDtypeStruct((tok, 3 * steps * w), BF),
            jax.ShapeDtypeStruct((3, tok, tok), BF),
        ],
        scratch_shapes=[pltpu.VMEM((3, tok, tok), BF)],
        compiler_params=params(dimension_semantics=("arbitrary",)),
        cost_estimate=cost(4 * tok * tok * width, 5 * tok * width),
        name="dispatch",
    )(routes, grad, grad)


def hidden_kernel(rows_ref, dl_ref, dr_ref, pre_ref, grad_ref, prob_ref, acc_l, acc_r):
    j = pl.program_id(0)
    half = rows_ref.shape[0]
    w = dl_ref.shape[1]
    hidden = dl_ref.shape[0]
    extra = rows_ref[:, 2 * w :]
    left = mm(jnp.concatenate([rows_ref[:, :w], extra], 0), dl_ref[...], ((1,), (1,)))
    right = mm(jnp.concatenate([rows_ref[:, w : 2 * w], extra], 0), dr_ref[...], ((1,), (1,)))

    @pl.when(j == 0)
    def _():
        acc_l[...] = left
        acc_r[...] = right

    @pl.when(j > 0)
    def _():
        acc_l[...] += left
        acc_r[...] += right

    @pl.when(j == pl.num_programs(0) - 1)
    def _():
        slots = pre_ref.shape[0]
        row = iota((2 * half, slots), 0)
        inner = row & (half - 1)
        group = inner >> 3
        source = group * 12 + jnp.where(row < half, inner & 7, 8 + (inner & 3))
        pick = as_bf(source == iota((2 * half, slots), 1))
        lane = iota((half, 128), 1)
        probs = jnp.zeros((half, 128), F32)
        for part in range(2):
            here = slice(part * half, (part + 1) * half)
            chosen = pick[here]
            gate = mm(chosen, pre_ref[:, :hidden])
            up = mm(chosen, pre_ref[:, hidden:])
            if part == 0:
                down = acc_l[here] + acc_r[here]
            else:
                low = (iota((half, hidden), 0) & 7) < 4
                mixed = jnp.where(low, acc_l[here], acc_r[here]).reshape(half // 8, 8, hidden)
                down = (mixed + pltpu.roll(mixed, 4, 1)).reshape(half, hidden)
            sigma = jax.nn.sigmoid(gate)
            swish = gate * sigma
            prob = jnp.sum(down * swish * up, axis=1, keepdims=True)
            probs = jnp.where(lane == part, prob, probs)
            grad_ref[here, :hidden] = (
                down * up * sigma * (1.0 + gate * (1.0 - sigma))
            ).astype(BF)
            grad_ref[here, hidden:] = (down * swish).astype(BF)
        prob_ref[...] = probs.astype(BF)


def hidden_grad(rows, down, pre):
    half = rows.shape[0]
    hidden, width = down.shape
    steps = 4
    w = width // (2 * steps)
    return pl.pallas_call(
        hidden_kernel,
        grid=(steps,),
        in_specs=[
            pl.BlockSpec((half, 3 * w), lambda j: (0, j)),
            pl.BlockSpec((hidden, w), lambda j: (0, j)),
            pl.BlockSpec((hidden, w), lambda j: (0, j + steps)),
            pl.BlockSpec(pre.shape, lambda j: (0, 0)),
        ],
        out_specs=[
            pl.BlockSpec((2 * half, 2 * hidden), lambda j: (0, 0)),
            pl.BlockSpec((half, 128), lambda j: (0, 0)),
        ],
        out_shape=[
            jax.ShapeDtypeStruct((2 * half, 2 * hidden), BF),
            jax.ShapeDtypeStruct((half, 128), BF),
        ],
        scratch_shapes=[pltpu.VMEM((2 * half, hidden), F32)] * 2,
        compiler_params=params(dimension_semantics=("arbitrary",)),
        cost_estimate=cost(4 * half * width * hidden, 2 * hidden * width),
        name="hidden_grad",
    )(rows, down, down, pre)


def columns_kernel(sizes, with_prob, *refs):
    grad_ref = refs[0]
    shards = refs[1 : 1 + sum(sizes)]
    out_ref = refs[-1]
    half = grad_ref.shape[0] // 2
    low = (iota((half, 128), 0) & 7) < 4
    at = 0
    for n, size in enumerate(sizes):
        parts = [r[...] for r in shards[at : at + size]]
        at += size
        shard = parts[0] if size == 1 else jnp.concatenate(parts, 0)
        out = mm(grad_ref[...], shard, ((1,), (1,)))
        out_ref[:, n * 384 : n * 384 + 256] = out[:half].astype(BF)
        out_ref[:, n * 384 + 256 : (n + 1) * 384] = jnp.where(
            low, out[half:, :128], out[half:, 128:]
        ).astype(BF)
    if with_prob:
        out_ref[:, len(sizes) * 384 :] = refs[-2][...]


def columns(grad, shards, prob):
    half = grad.shape[0] // 2
    sizes = tuple(len(s) for s in shards)
    flat = [r for s in shards for r in s]
    wide = 384 * len(shards) + (0 if prob is None else 128)
    rest = [] if prob is None else [prob]
    return pl.pallas_call(
        functools.partial(columns_kernel, sizes, prob is not None),
        out_shape=jax.ShapeDtypeStruct((half, wide), BF),
        compiler_params=params(),
        cost_estimate=cost(
            2 * grad.size * 256 * len(shards), 2 * (grad.size + 256 * grad.shape[1] * len(shards))
        ),
        name="columns",
    )(grad, *flat, *rest)


def combine_kernel(counts, first, ids_ref, mask_ref, gate_ref, *refs):
    if first:
        arrived, (out_ref, prob_ref) = refs[:-2], refs[-2:]
    else:
        before, arrived, out_ref = refs[0], refs[1:-1], refs[-1]
        out_ref[...] = before[...]
    main_mask, low, high = mask_ref[0], mask_ref[1], mask_ref[2]
    gate = gate_ref[...]
    place = 0
    for ref, count in zip(arrived, counts):
        for k in range(count):
            main = ref[:, k * 384 : k * 384 + 256]
            extra = ref[:, k * 384 + 256 : (k + 1) * 384]
            picked = mm(main_mask, main) + jnp.concatenate([mm(low, extra), mm(high, extra)], 1)
            where = pl.multiple_of(ids_ref[place] * 256, 256)
            out_ref[:, pl.ds(where, 256)] = (gate * picked).astype(BF)
            place += 1
    if first:
        probs = arrived[0][:, counts[0] * 384 :]
        prob_ref[...] = (mm(main_mask, probs)[:, :1] + mm(low, probs)[:, 1:2]).astype(BF)


def combine(ids, masks, gate, before, arrived, counts, width):
    tok = gate.shape[0]
    first = before is None
    vmem = pl.BlockSpec(memory_space=pltpu.VMEM)
    operands = ([] if first else [before]) + list(arrived)
    out_shape = [jax.ShapeDtypeStruct((tok, width), BF)]
    if first:
        out_shape.append(jax.ShapeDtypeStruct((tok, 1), BF))
    return pl.pallas_call(
        functools.partial(combine_kernel, counts, first),
        in_specs=[pl.BlockSpec(memory_space=pltpu.SMEM)] + [vmem] * (2 + len(operands)),
        out_specs=[vmem] * len(out_shape),
        out_shape=out_shape,
        compiler_params=params(),
        cost_estimate=cost(4 * tok * tok * 256 * sum(counts), 6 * tok * width),
        name="combine",
    )(ids, masks, gate, *operands)


def delta_kernel(grad_ref, out_ref, delta_ref):
    heads = delta_ref.shape[0]
    for h in range(heads):
        cols = slice(h * HEAD, (h + 1) * HEAD)
        product = grad_ref[:, cols].astype(F32) * out_ref[:, cols].astype(F32)
        delta_ref[h : h + 1, :] = jnp.sum(product.T, axis=0, keepdims=True)


def deltas(grad, out):
    tok, width = grad.shape
    return pl.pallas_call(
        delta_kernel,
        out_shape=jax.ShapeDtypeStruct((width // HEAD, tok), F32),
        compiler_params=params(),
        cost_estimate=cost(2 * tok * width, 4 * tok * width),
        name="deltas",
    )(grad, out)


def attend_kernel(first, last, pairs, start, place_ref, *refs):
    q_ref, g_ref, qo_ref, go_ref, d_ref, do_ref = refs[:6]
    kv = refs[6:14]
    at = 14
    if not first:
        turned, before = refs[at : at + 2]
        at += 4
    dq_ref, dqo_ref = refs[at : at + 2]
    at += 2
    if first:
        turned = refs[at]
        at += 1
    if last:
        sent_ref = refs[at]
        at += 1
    sums, kept, low_probs, low_grads = refs[at : at + 4]
    i = pl.program_id(0)
    chip, core = place_ref[0], place_ref[1]
    tok = q_ref.shape[0]
    block = 2 * tok
    rows = 2 * block
    scale = HEAD**-0.5
    factor = scale * LOG2E
    n_heads = do_ref.shape[0]
    valid = [None] + [chip >= s for s in range(1, 5)] + [chip + s >= 8 for s in range(1, 4)]

    @pl.when(i == 0)
    def _():
        if first:
            sums[...] = jnp.zeros_like(sums)
            for s in range(8):
                turned[:, s * block : (s + 1) * block] = kv[s][:, :HEAD].T
        else:
            sums[...] = before[...]

    def stack(own, other):
        return jnp.concatenate(
            [own[:, :HEAD], other[:, :HEAD], own[:, HEAD:], other[:, HEAD:]], 0
        )

    query = stack(q_ref, qo_ref)
    grad = stack(g_ref, go_ref)
    head = start + 2 * i
    delta = jnp.concatenate(
        [
            r[pl.ds(at_head, 1), :]
            for n in range(2)
            for r, at_head in ((d_ref, core * n_heads + head + n), (do_ref, head + n))
        ],
        1,
    )
    highest = total = None
    bases = []
    for s in range(8):
        here = slice(s * block, (s + 1) * block)
        scores = mm(kv[s][:, :HEAD], query, ((1,), (1,)))
        if s == 0:
            flip = core * tok
            key_pos = iota((block, rows), 0) ^ flip
            row_pos = (iota((block, rows), 1) & (block - 1)) ^ flip
            scores = jnp.where(key_pos <= row_pos, scores, -1e30)
        top = jnp.max(scores, axis=0, keepdims=True)
        if s == 0:
            new = base = top
        else:
            new = jnp.maximum(highest, jnp.where(valid[s], top, -1e30))
            base = jnp.where(valid[s], new, 1e30)
        expo = jnp.exp2((scores - base) * factor)
        kept[here, :] = expo
        fresh = jnp.sum(expo, axis=0, keepdims=True)
        total = fresh if s == 0 else total * jnp.exp2((highest - new) * factor) + fresh
        highest = new
        bases.append(new)
    inverse = 1.0 / total
    for s in range(8):
        here = slice(s * block, (s + 1) * block)
        share = inverse * jnp.exp2((bases[s] - highest) * factor)
        probs = kept[here, :] * share
        part = mm(kv[s][:, HEAD:], grad, ((1,), (1,)))
        low_grads[here, :] = (probs * (part - delta)).astype(BF)
        low_probs[here, :] = probs.astype(BF)
    sums[:, HEAD:] += mm(low_probs[...], grad)
    sums[:, :HEAD] += mm(low_grads[...], query)
    dq = (mm(turned[...], low_grads[...]) * scale).T.astype(BF)
    for n in range(2):
        cols = slice(n * HEAD, (n + 1) * HEAD)
        dq_ref[:, cols] = dq[n * block : n * block + tok]
        dqo_ref[:, cols] = dq[n * block + tok : (n + 1) * block]

    if last:

        @pl.when(i == pairs - 1)
        def _():
            for s in range(8):
                source = lax.rem(chip + (8 - s if s < 5 else s - 4), 8)
                to = pl.ds(pl.multiple_of(source * block, block), block)
                sent_ref[to, :] = sums[s * block : (s + 1) * block, :]


def attend(first, last, start, heads, place, queries, grads, others, delta, delta_other, kv, carry):
    tok, width = queries.shape
    n_heads = width // HEAD // 2
    pairs = heads // 2
    pair = (tok, 2 * HEAD)
    block, rows = 2 * tok, 4 * tok
    lead = start // 2

    def whole(a):
        return pl.BlockSpec(a.shape, lambda i, p: (0,) * len(a.shape))

    half_pairs = n_heads // 2
    sums = jax.ShapeDtypeStruct((8 * block, 2 * HEAD), F32)
    turned = jax.ShapeDtypeStruct((HEAD, 8 * block), BF)
    out_shape = [
        jax.ShapeDtypeStruct((tok, width), BF),
        jax.ShapeDtypeStruct((tok, width // 2), BF),
    ]
    out_specs = [
        pl.BlockSpec(pair, lambda i, p: (0, p[1] * half_pairs + lead + i)),
        pl.BlockSpec(pair, lambda i, p: (0, lead + i)),
    ]
    scratch = [
        pltpu.VMEM((8 * block, rows), F32),
        pltpu.VMEM((8 * block, rows), BF),
        pltpu.VMEM((8 * block, rows), BF),
    ]
    extra = []
    if first:
        extra.append(turned)
    if last:
        extra.append(sums)
        scratch = [pltpu.VMEM(sums.shape, F32)] + scratch
    else:
        extra.append(sums)
    mine = pl.BlockSpec(pair, lambda i, p: (0, p[1] * half_pairs + lead + i))
    in_specs = [
        mine,
        mine,
        pl.BlockSpec(pair, lambda i, p: (0, lead + i)),
        pl.BlockSpec(pair, lambda i, p: (0, half_pairs + lead + i)),
        whole(delta),
        whole(delta_other),
    ]
    in_specs += [whole(a) for a in kv]
    more = list(kv)
    alias = {}
    if not first:
        in_specs += [whole(a) for a in carry[:2]] + [pl.BlockSpec(memory_space=pl.ANY)] * 2
        more += list(carry)
        alias = {17: 0, 18: 1}
    return pl.pallas_call(
        functools.partial(attend_kernel, first, last, pairs, start),
        grid_spec=pltpu.PrefetchScalarGridSpec(
            num_scalar_prefetch=1,
            grid=(pairs,),
            in_specs=in_specs,
            out_specs=out_specs + [whole(a) for a in extra],
            scratch_shapes=scratch,
        ),
        out_shape=out_shape + extra,
        input_output_aliases=alias,
        compiler_params=params(60, dimension_semantics=("arbitrary",)),
        cost_estimate=cost(
            40 * heads * 8 * block * block * HEAD, 12 * tok * width, heads * 8 * block * block
        ),
        name="attend",
    )(place, queries, grads, others, others, delta, delta_other, *more)


def hold(x, until):
    return lax.optimization_barrier((x, until))[0]


def along(x, step):
    return lax.ppermute(x, "ctx", [(i, (i + 2 * step) % 16) for i in range(16)])


def swap(x):
    return lax.ppermute(x, "ctx", [(i, i ^ 1) for i in range(16)])


def exchange(x):
    groups = lax.axis_size("exp")
    cut = x.reshape(groups, x.shape[0] // groups, x.shape[1])
    out = lax.all_to_all(cut, "exp", split_axis=0, concat_axis=0, tiled=True)
    return out.reshape(x.shape)


def body(
    grad_out,
    routes,
    gate_probs,
    saved_pre,
    down_weight,
    gate_up_weight,
    queries,
    keys_values,
    attn_grad,
    attn_out,
):
    width = grad_out.shape[2]
    index = lax.axis_index("ctx")
    chip, core = index // 2, index % 2
    place = jnp.stack([chip, core]).astype(jnp.int32)
    query, grad, kv_rows = queries[0], attn_grad[0], keys_values[0]
    half = width // 2

    def mine(x, n):
        return lax.dynamic_slice_in_dim(x, core * n, n, 1)

    def theirs(x, n):
        return lax.dynamic_slice_in_dim(x, (1 - core) * n, n, 1)

    own = jnp.concatenate([mine(kv_rows, 2 * HEAD), swap(theirs(kv_rows, 2 * HEAD))], 0)
    up, down = [own], [own]
    for s in range(4):
        up.append(along(up[-1], 1))
        if s < 3:
            down.append(along(down[-1], -1))
    kv = up + down[1:]

    send, masks = dispatch(routes[0], grad_out[0])
    arrived = exchange(send)

    full_down = lax.all_gather(down_weight[0], "ctx", axis=1, tiled=True)
    shard = gate_up_weight[0]
    begin = hold(shard, (up[3], down[3]))
    fore, back = [begin], [begin]
    for s in range(3):
        fore.append(along(fore[-1], 1))
        back.append(along(back[-1], -1))
    mid = shard.shape[0] // 2
    last = (along(fore[3][:mid], 1), along(back[3][mid:], -1))
    steps = [[((shard,), chip, core), ((swap(shard),), chip, 1 - core)]]
    for s in range(1, 4):
        steps.append(
            [
                ((fore[s],), chip - s, core),
                ((back[s],), chip + s, core),
                ((swap(fore[s]),), chip - s, 1 - core),
                ((swap(back[s]),), chip + s, 1 - core),
            ]
        )
    steps.append(
        [(last, chip + 4, core), (tuple(swap(x) for x in last), chip + 4, 1 - core)]
    )

    delta = deltas(grad, attn_out[0])
    query_late, grad_late = hold((query, grad), up[0])
    others = swap(jnp.concatenate([theirs(query_late, half), theirs(grad_late, half)], 1))
    n_heads = delta.shape[0] // 2
    delta_other = swap(lax.dynamic_slice_in_dim(delta, (1 - core) * n_heads, n_heads, 0))
    carry = None
    for n, heads in enumerate(PARTS):
        begun, ended = n == 0, n == len(PARTS) - 1
        operands = (query, grad, others, delta, delta_other)
        if n == 0:
            operands = hold(operands, send)
        if ended:
            operands = hold(operands, arrived)
        if n in HOLD:
            operands = hold(operands, (fore[HOLD[n]], back[HOLD[n]]))
        outs = attend(begun, ended, sum(PARTS[:n]), heads, place, *operands, kv, carry)
        if begun:
            turned = outs[2]
        carry = (turned, outs[-1], outs[0], outs[1])
    query_grad, dq_other = outs[:2]
    terms = outs[-1]
    dq_back = swap(dq_other)
    chips = [[2 * z + c for z in range(8)] for c in range(2)]
    kv_sum = lax.psum_scatter(
        hold(terms, (fore[3], back[3])), "ctx", scatter_dimension=0, tiled=True, axis_index_groups=chips
    )

    arrived = hold(arrived, terms)
    hidden, prob = hidden_grad(arrived, full_down, saved_pre[0, 0])
    back_rows, counts, ids = [], [], []
    for n, group in enumerate(GROUPS):
        members = [m for s in group for m in steps[s]]
        source = hidden
        if n == 0:
            source = hold(hidden, (fore[3], back[3]))
        if n == 1:
            source = hold(hidden, out)
        out = columns(source, [m[0] for m in members], prob if n == 0 else None)
        if n == 0:
            out = hold(out, last)
        back_rows.append(exchange(out))
        counts.append(len(members))
        ids.append(
            jnp.stack([((m[1] + 8) % 8) * 2 + m[2] for m in members]).astype(jnp.int32)
        )
    moe_grad, prob_grad = combine(
        jnp.concatenate(ids[:-1]), masks, gate_probs[0], None, back_rows[:-1], tuple(counts[:-1]), width
    )
    (moe_grad,) = combine(
        ids[-1], masks, gate_probs[0], moe_grad, back_rows[-1:], tuple(counts[-1:]), width
    )

    kv_sum, dq_back = hold((kv_sum, dq_back), prob_grad)
    query_grad = lax.dynamic_update_slice(query_grad, dq_back, (0, (1 - core) * half))
    factor = jnp.where(jnp.arange(2 * HEAD) < HEAD, F32(HEAD**-0.5), F32(1.0))
    summed = (kv_sum.astype(F32) * factor).astype(BF)
    tok = kv_rows.shape[0]
    kv_own, kv_back = summed[:tok], swap(summed[tok:])
    kv_grad = jnp.where(
        core == 0,
        jnp.concatenate([kv_own, kv_back], 1),
        jnp.concatenate([kv_back, kv_own], 1),
    )
    return moe_grad[None], prob_grad[None], query_grad[None], kv_grad[None]


def solution(mesh):
    tokens = P("exp", "ctx", None)
    placed = (
        tokens,
        tokens,
        tokens,
        P("ctx", "exp", None, None),
        P("exp", None, "ctx"),
        tokens,
        tokens,
        tokens,
        tokens,
        tokens,
    )
    return jax.shard_map(
        body,
        mesh=mesh,
        in_specs=placed,
        out_specs=(tokens, tokens, tokens, tokens),
        check_vma=False,
    )
```

```python
import functools

import jax
import jax.numpy as jnp
from jax import lax
from jax.experimental import pallas as pl
from jax.experimental.pallas import tpu as pltpu
from jax.sharding import PartitionSpec as P

HEAD = 128
BF, F32 = jnp.bfloat16, jnp.float32
LOG2E = 1.4426950408889634
GROUPS = ((0, 1), (2, 3, 4))
PARTS = (4, 4, 4, 4)
HOLD = {2: 1}


def mm(a, b, dims=((1,), (0,))):
    return lax.dot_general(a, b, (dims, ((), ())), preferred_element_type=F32)


def iota(shape, dim):
    return lax.broadcasted_iota(jnp.int32, shape, dim)


def as_bf(mask):
    return jnp.where(mask, 1.0, 0.0).astype(BF)


def params(mib=48, **kw):
    return pltpu.CompilerParams(vmem_limit_bytes=mib * 1024 * 1024, **kw)


def cost(flops, nbytes, exps=0):
    return pl.CostEstimate(flops=flops, bytes_accessed=nbytes, transcendentals=exps)


def dispatch_kernel(routes_ref, left_ref, right_ref, send_ref, mask_ref, turned):
    @pl.when(pl.program_id(0) == 0)
    def _():
        tok = routes_ref.shape[0]
        route = routes_ref[...]
        lane = iota((tok, tok), 1)
        hot = route == lane
        lower = iota((tok, tok), 0) > lane
        earlier = mm(as_bf(lower), as_bf(hot))
        slot = jnp.sum(jnp.where(hot, earlier, 0.0), axis=1, keepdims=True).astype(jnp.int32)
        first = jnp.where(slot < 8, route * 8 + slot, -1)
        second = jnp.where(slot < 8, -8, route * 8 + slot - 8)
        for i, key in enumerate((first, second, second + 4)):
            one = jnp.where(key == lane, 1.0, 0.0)
            mask_ref[i] = one.astype(BF)
            turned[i] = one.T.astype(BF)

    left, right = left_ref[...], right_ref[...]
    w = left.shape[1]
    send_ref[:, :w] = mm(turned[0], left).astype(BF)
    send_ref[:, w : 2 * w] = mm(turned[0], right).astype(BF)
    send_ref[:, 2 * w :] = (mm(turned[1], left) + mm(turned[2], right)).astype(BF)


def dispatch(routes, grad):
    tok, width = grad.shape
    steps = 4
    w = width // (2 * steps)
    return pl.pallas_call(
        dispatch_kernel,
        grid=(steps,),
        in_specs=[
            pl.BlockSpec((tok, 1), lambda j: (0, 0)),
            pl.BlockSpec((tok, w), lambda j: (0, j)),
            pl.BlockSpec((tok, w), lambda j: (0, j + steps)),
        ],
        out_specs=[
            pl.BlockSpec((tok, 3 * w), lambda j: (0, j)),
            pl.BlockSpec((3, tok, tok), lambda j: (0, 0, 0)),
        ],
        out_shape=[
            jax.ShapeDtypeStruct((tok, 3 * steps * w), BF),
            jax.ShapeDtypeStruct((3, tok, tok), BF),
        ],
        scratch_shapes=[pltpu.VMEM((3, tok, tok), BF)],
        compiler_params=params(dimension_semantics=("arbitrary",)),
        cost_estimate=cost(4 * tok * tok * width, 5 * tok * width),
        name="dispatch",
    )(routes, grad, grad)


def hidden_kernel(rows_ref, dl_ref, dr_ref, pre_ref, grad_ref, prob_ref, acc_l, acc_r):
    j = pl.program_id(0)
    half = rows_ref.shape[0]
    w = dl_ref.shape[1]
    hidden = dl_ref.shape[0]
    extra = rows_ref[:, 2 * w :]
    left = mm(jnp.concatenate([rows_ref[:, :w], extra], 0), dl_ref[...], ((1,), (1,)))
    right = mm(jnp.concatenate([rows_ref[:, w : 2 * w], extra], 0), dr_ref[...], ((1,), (1,)))

    @pl.when(j == 0)
    def _():
        acc_l[...] = left
        acc_r[...] = right

    @pl.when(j > 0)
    def _():
        acc_l[...] += left
        acc_r[...] += right

    @pl.when(j == pl.num_programs(0) - 1)
    def _():
        slots = pre_ref.shape[0]
        row = iota((2 * half, slots), 0)
        inner = row & (half - 1)
        group = inner >> 3
        source = group * 12 + jnp.where(row < half, inner & 7, 8 + (inner & 3))
        pick = as_bf(source == iota((2 * half, slots), 1))
        lane = iota((half, 128), 1)
        probs = jnp.zeros((half, 128), F32)
        for part in range(2):
            here = slice(part * half, (part + 1) * half)
            chosen = pick[here]
            gate = mm(chosen, pre_ref[:, :hidden])
            up = mm(chosen, pre_ref[:, hidden:])
            if part == 0:
                down = acc_l[here] + acc_r[here]
            else:
                low = (iota((half, hidden), 0) & 7) < 4
                mixed = jnp.where(low, acc_l[here], acc_r[here]).reshape(half // 8, 8, hidden)
                down = (mixed + pltpu.roll(mixed, 4, 1)).reshape(half, hidden)
            sigma = jax.nn.sigmoid(gate)
            swish = gate * sigma
            prob = jnp.sum(down * swish * up, axis=1, keepdims=True)
            probs = jnp.where(lane == part, prob, probs)
            grad_ref[here, :hidden] = (
                down * up * sigma * (1.0 + gate * (1.0 - sigma))
            ).astype(BF)
            grad_ref[here, hidden:] = (down * swish).astype(BF)
        prob_ref[...] = probs.astype(BF)


def hidden_grad(rows, down, pre):
    half = rows.shape[0]
    hidden, width = down.shape
    steps = 4
    w = width // (2 * steps)
    return pl.pallas_call(
        hidden_kernel,
        grid=(steps,),
        in_specs=[
            pl.BlockSpec((half, 3 * w), lambda j: (0, j)),
            pl.BlockSpec((hidden, w), lambda j: (0, j)),
            pl.BlockSpec((hidden, w), lambda j: (0, j + steps)),
            pl.BlockSpec(pre.shape, lambda j: (0, 0)),
        ],
        out_specs=[
            pl.BlockSpec((2 * half, 2 * hidden), lambda j: (0, 0)),
            pl.BlockSpec((half, 128), lambda j: (0, 0)),
        ],
        out_shape=[
            jax.ShapeDtypeStruct((2 * half, 2 * hidden), BF),
            jax.ShapeDtypeStruct((half, 128), BF),
        ],
        scratch_shapes=[pltpu.VMEM((2 * half, hidden), F32)] * 2,
        compiler_params=params(dimension_semantics=("arbitrary",)),
        cost_estimate=cost(4 * half * width * hidden, 2 * hidden * width),
        name="hidden_grad",
    )(rows, down, down, pre)


def columns_kernel(sizes, with_prob, *refs):
    grad_ref = refs[0]
    shards = refs[1 : 1 + sum(sizes)]
    out_ref = refs[-1]
    half = grad_ref.shape[0] // 2
    low = (iota((half, 128), 0) & 7) < 4
    at = 0
    for n, size in enumerate(sizes):
        parts = [r[...] for r in shards[at : at + size]]
        at += size
        shard = parts[0] if size == 1 else jnp.concatenate(parts, 0)
        out = mm(grad_ref[...], shard, ((1,), (1,)))
        out_ref[:, n * 384 : n * 384 + 256] = out[:half].astype(BF)
        out_ref[:, n * 384 + 256 : (n + 1) * 384] = jnp.where(
            low, out[half:, :128], out[half:, 128:]
        ).astype(BF)
    if with_prob:
        out_ref[:, len(sizes) * 384 :] = refs[-2][...]


def columns(grad, shards, prob):
    half = grad.shape[0] // 2
    sizes = tuple(len(s) for s in shards)
    flat = [r for s in shards for r in s]
    wide = 384 * len(shards) + (0 if prob is None else 128)
    rest = [] if prob is None else [prob]
    return pl.pallas_call(
        functools.partial(columns_kernel, sizes, prob is not None),
        out_shape=jax.ShapeDtypeStruct((half, wide), BF),
        compiler_params=params(),
        cost_estimate=cost(
            2 * grad.size * 256 * len(shards), 2 * (grad.size + 256 * grad.shape[1] * len(shards))
        ),
        name="columns",
    )(grad, *flat, *rest)


def combine_kernel(counts, first, ids_ref, mask_ref, gate_ref, *refs):
    if first:
        arrived, (out_ref, prob_ref) = refs[:-2], refs[-2:]
    else:
        before, arrived, out_ref = refs[0], refs[1:-1], refs[-1]
        out_ref[...] = before[...]
    main_mask, low, high = mask_ref[0], mask_ref[1], mask_ref[2]
    gate = gate_ref[...]
    place = 0
    for ref, count in zip(arrived, counts):
        for k in range(count):
            main = ref[:, k * 384 : k * 384 + 256]
            extra = ref[:, k * 384 + 256 : (k + 1) * 384]
            picked = mm(main_mask, main) + jnp.concatenate([mm(low, extra), mm(high, extra)], 1)
            where = pl.multiple_of(ids_ref[place] * 256, 256)
            out_ref[:, pl.ds(where, 256)] = (gate * picked).astype(BF)
            place += 1
    if first:
        probs = arrived[0][:, counts[0] * 384 :]
        prob_ref[...] = (mm(main_mask, probs)[:, :1] + mm(low, probs)[:, 1:2]).astype(BF)


def combine(ids, masks, gate, before, arrived, counts, width):
    tok = gate.shape[0]
    first = before is None
    vmem = pl.BlockSpec(memory_space=pltpu.VMEM)
    operands = ([] if first else [before]) + list(arrived)
    out_shape = [jax.ShapeDtypeStruct((tok, width), BF)]
    if first:
        out_shape.append(jax.ShapeDtypeStruct((tok, 1), BF))
    return pl.pallas_call(
        functools.partial(combine_kernel, counts, first),
        in_specs=[pl.BlockSpec(memory_space=pltpu.SMEM)] + [vmem] * (2 + len(operands)),
        out_specs=[vmem] * len(out_shape),
        out_shape=out_shape,
        compiler_params=params(),
        cost_estimate=cost(4 * tok * tok * 256 * sum(counts), 6 * tok * width),
        name="combine",
    )(ids, masks, gate, *operands)


def delta_kernel(grad_ref, out_ref, delta_ref):
    heads = delta_ref.shape[0]
    for h in range(heads):
        cols = slice(h * HEAD, (h + 1) * HEAD)
        product = grad_ref[:, cols].astype(F32) * out_ref[:, cols].astype(F32)
        delta_ref[h : h + 1, :] = jnp.sum(product.T, axis=0, keepdims=True)


def deltas(grad, out):
    tok, width = grad.shape
    return pl.pallas_call(
        delta_kernel,
        out_shape=jax.ShapeDtypeStruct((width // HEAD, tok), F32),
        compiler_params=params(),
        cost_estimate=cost(2 * tok * width, 4 * tok * width),
        name="deltas",
    )(grad, out)


def attend_kernel(first, last, pairs, start, place_ref, *refs):
    q_ref, g_ref, qo_ref, go_ref, d_ref, do_ref = refs[:6]
    kv = refs[6:14]
    at = 14
    if not first:
        turned, before = refs[at : at + 2]
        at += 4
    dq_ref, dqo_ref = refs[at : at + 2]
    at += 2
    if first:
        turned = refs[at]
        at += 1
    if last:
        sent_ref = refs[at]
        at += 1
    sums, kept, low_probs, low_grads = refs[at : at + 4]
    i = pl.program_id(0)
    chip, core = place_ref[0], place_ref[1]
    tok = q_ref.shape[0]
    block = 2 * tok
    rows = 2 * block
    scale = HEAD**-0.5
    factor = scale * LOG2E
    n_heads = do_ref.shape[0]
    valid = [None] + [chip >= s for s in range(1, 5)] + [chip + s >= 8 for s in range(1, 4)]

    @pl.when(i == 0)
    def _():
        if first:
            sums[...] = jnp.zeros_like(sums)
            for s in range(8):
                turned[:, s * block : (s + 1) * block] = kv[s][:, :HEAD].T
        else:
            sums[...] = before[...]

    def stack(own, other):
        return jnp.concatenate(
            [own[:, :HEAD], other[:, :HEAD], own[:, HEAD:], other[:, HEAD:]], 0
        )

    query = stack(q_ref, qo_ref)
    grad = stack(g_ref, go_ref)
    head = start + 2 * i
    delta = jnp.concatenate(
        [
            r[pl.ds(at_head, 1), :]
            for n in range(2)
            for r, at_head in ((d_ref, core * n_heads + head + n), (do_ref, head + n))
        ],
        1,
    )
    highest = total = None
    bases = []
    for s in range(8):
        here = slice(s * block, (s + 1) * block)
        scores = mm(kv[s][:, :HEAD], query, ((1,), (1,)))
        if s == 0:
            flip = core * tok
            key_pos = iota((block, rows), 0) ^ flip
            row_pos = (iota((block, rows), 1) & (block - 1)) ^ flip
            scores = jnp.where(key_pos <= row_pos, scores, -1e30)
        top = jnp.max(scores, axis=0, keepdims=True)
        if s == 0:
            new = base = top
        else:
            new = jnp.maximum(highest, jnp.where(valid[s], top, -1e30))
            base = jnp.where(valid[s], new, 1e30)
        expo = jnp.exp2((scores - base) * factor)
        kept[here, :] = expo
        fresh = jnp.sum(expo, axis=0, keepdims=True)
        total = fresh if s == 0 else total * jnp.exp2((highest - new) * factor) + fresh
        highest = new
        bases.append(new)
    inverse = 1.0 / total
    for s in range(8):
        here = slice(s * block, (s + 1) * block)
        share = inverse * jnp.exp2((bases[s] - highest) * factor)
        probs = kept[here, :] * share
        part = mm(kv[s][:, HEAD:], grad, ((1,), (1,)))
        low_grads[here, :] = (probs * (part - delta)).astype(BF)
        low_probs[here, :] = probs.astype(BF)
    sums[:, HEAD:] += mm(low_probs[...], grad)
    sums[:, :HEAD] += mm(low_grads[...], query)
    dq = (mm(turned[...], low_grads[...]) * scale).T.astype(BF)
    for n in range(2):
        cols = slice(n * HEAD, (n + 1) * HEAD)
        dq_ref[:, cols] = dq[n * block : n * block + tok]
        dqo_ref[:, cols] = dq[n * block + tok : (n + 1) * block]

    if last:

        @pl.when(i == pairs - 1)
        def _():
            for s in range(8):
                source = lax.rem(chip + (8 - s if s < 5 else s - 4), 8)
                to = pl.ds(pl.multiple_of(source * block, block), block)
                sent_ref[to, :] = sums[s * block : (s + 1) * block, :]


def attend(first, last, start, heads, place, queries, grads, others, delta, delta_other, kv, carry):
    tok, width = queries.shape
    n_heads = width // HEAD // 2
    pairs = heads // 2
    pair = (tok, 2 * HEAD)
    block, rows = 2 * tok, 4 * tok
    lead = start // 2

    def whole(a):
        return pl.BlockSpec(a.shape, lambda i, p: (0,) * len(a.shape))

    half_pairs = n_heads // 2
    sums = jax.ShapeDtypeStruct((8 * block, 2 * HEAD), F32)
    turned = jax.ShapeDtypeStruct((HEAD, 8 * block), BF)
    out_shape = [
        jax.ShapeDtypeStruct((tok, width), BF),
        jax.ShapeDtypeStruct((tok, width // 2), BF),
    ]
    out_specs = [
        pl.BlockSpec(pair, lambda i, p: (0, p[1] * half_pairs + lead + i)),
        pl.BlockSpec(pair, lambda i, p: (0, lead + i)),
    ]
    scratch = [
        pltpu.VMEM((8 * block, rows), F32),
        pltpu.VMEM((8 * block, rows), BF),
        pltpu.VMEM((8 * block, rows), BF),
    ]
    extra = []
    if first:
        extra.append(turned)
    if last:
        extra.append(sums)
        scratch = [pltpu.VMEM(sums.shape, F32)] + scratch
    else:
        extra.append(sums)
    mine = pl.BlockSpec(pair, lambda i, p: (0, p[1] * half_pairs + lead + i))
    in_specs = [
        mine,
        mine,
        pl.BlockSpec(pair, lambda i, p: (0, lead + i)),
        pl.BlockSpec(pair, lambda i, p: (0, half_pairs + lead + i)),
        whole(delta),
        whole(delta_other),
    ]
    in_specs += [whole(a) for a in kv]
    more = list(kv)
    alias = {}
    if not first:
        in_specs += [whole(a) for a in carry[:2]] + [pl.BlockSpec(memory_space=pl.ANY)] * 2
        more += list(carry)
        alias = {17: 0, 18: 1}
    return pl.pallas_call(
        functools.partial(attend_kernel, first, last, pairs, start),
        grid_spec=pltpu.PrefetchScalarGridSpec(
            num_scalar_prefetch=1,
            grid=(pairs,),
            in_specs=in_specs,
            out_specs=out_specs + [whole(a) for a in extra],
            scratch_shapes=scratch,
        ),
        out_shape=out_shape + extra,
        input_output_aliases=alias,
        compiler_params=params(60, dimension_semantics=("arbitrary",)),
        cost_estimate=cost(
            40 * heads * 8 * block * block * HEAD, 12 * tok * width, heads * 8 * block * block
        ),
        name="attend",
    )(place, queries, grads, others, others, delta, delta_other, *more)


def hold(x, until):
    return lax.optimization_barrier((x, until))[0]


def along(x, step):
    return lax.ppermute(x, "ctx", [(i, (i + 2 * step) % 16) for i in range(16)])


def swap(x):
    return lax.ppermute(x, "ctx", [(i, i ^ 1) for i in range(16)])


def exchange(x):
    groups = lax.axis_size("exp")
    cut = x.reshape(groups, x.shape[0] // groups, x.shape[1])
    out = lax.all_to_all(cut, "exp", split_axis=0, concat_axis=0, tiled=True)
    return out.reshape(x.shape)


def body(
    grad_out,
    routes,
    gate_probs,
    saved_pre,
    down_weight,
    gate_up_weight,
    queries,
    keys_values,
    attn_grad,
    attn_out,
):
    width = grad_out.shape[2]
    index = lax.axis_index("ctx")
    chip, core = index // 2, index % 2
    place = jnp.stack([chip, core]).astype(jnp.int32)
    query, grad, kv_rows = queries[0], attn_grad[0], keys_values[0]
    half = width // 2

    def mine(x, n):
        return lax.dynamic_slice_in_dim(x, core * n, n, 1)

    def theirs(x, n):
        return lax.dynamic_slice_in_dim(x, (1 - core) * n, n, 1)

    own = jnp.concatenate([mine(kv_rows, 2 * HEAD), swap(theirs(kv_rows, 2 * HEAD))], 0)
    up, down = [own], [own]
    for s in range(4):
        up.append(along(up[-1], 1))
        if s < 3:
            down.append(along(down[-1], -1))
    kv = up + down[1:]

    send, masks = dispatch(routes[0], grad_out[0])
    arrived = exchange(send)

    full_down = lax.all_gather(down_weight[0], "ctx", axis=1, tiled=True)
    shard = gate_up_weight[0]
    begin = hold(shard, (up[3], down[3]))
    shard_now = begin
    fore, back = [begin], [begin]
    fore.append(along(shard_now, 1))
    back.append(along(shard_now, -1))

    delta = deltas(grad, attn_out[0])
    query_late, grad_late = hold((query, grad), up[0])
    others = swap(jnp.concatenate([theirs(query_late, half), theirs(grad_late, half)], 1))
    n_heads = delta.shape[0] // 2
    delta_other = swap(lax.dynamic_slice_in_dim(delta, (1 - core) * n_heads, n_heads, 0))
    carry = None
    for n, heads in enumerate(PARTS):
        begun, ended = n == 0, n == len(PARTS) - 1
        operands = (query, grad, others, delta, delta_other)
        if n == 0:
            operands = hold(operands, send)
        if n == 2:
            fore[1], back[1] = hold((fore[1], back[1]), outs[-1])
            for s in range(2):
                fore.append(along(fore[-1], 1))
                back.append(along(back[-1], -1))
            mid = shard.shape[0] // 2
            last = (along(fore[3][:mid], 1), along(back[3][mid:], -1))
            steps = [[((shard,), chip, core), ((swap(shard),), chip, 1 - core)]]
            for s in range(1, 4):
                steps.append(
                    [
                        ((fore[s],), chip - s, core),
                        ((back[s],), chip + s, core),
                        ((swap(fore[s]),), chip - s, 1 - core),
                        ((swap(back[s]),), chip + s, 1 - core),
                    ]
                )
            steps.append(
                [(last, chip + 4, core), (tuple(swap(x) for x in last), chip + 4, 1 - core)]
            )
        if ended:
            hidden, prob = hidden_grad(hold(arrived, outs[-1]), full_down, saved_pre[0, 0])
            near = columns(hidden, [m[0] for g in GROUPS[0] for m in steps[g]], prob)
            near_back = exchange(near)
            operands = hold(operands, near)
        if n in HOLD:
            operands = hold(operands, (fore[HOLD[n]], back[HOLD[n]]))
        outs = attend(begun, ended, sum(PARTS[:n]), heads, place, *operands, kv, carry)
        if begun:
            turned = outs[2]
        carry = (turned, outs[-1], outs[0], outs[1])
    query_grad, dq_other = outs[:2]
    terms = outs[-1]
    dq_back = swap(dq_other)
    chips = [[2 * z + c for z in range(8)] for c in range(2)]
    kv_sum = lax.psum_scatter(
        hold(terms, (fore[3], back[3], near_back)), "ctx", scatter_dimension=0, tiled=True, axis_index_groups=chips
    )

    back_rows, counts, ids = [], [], []
    for n, group in enumerate(GROUPS):
        members = [m for s in group for m in steps[s]]
        if n == 0:
            back_rows.append(near_back)
        else:
            source = hold(hidden, (terms, near_back))
            out = columns(source, [m[0] for m in members], None)
            back_rows.append(exchange(out))
        counts.append(len(members))
        ids.append(
            jnp.stack([((m[1] + 8) % 8) * 2 + m[2] for m in members]).astype(jnp.int32)
        )
    moe_grad, prob_grad = combine(
        jnp.concatenate(ids[:-1]), masks, gate_probs[0], None, back_rows[:-1], tuple(counts[:-1]), width
    )
    (moe_grad,) = combine(
        ids[-1], masks, gate_probs[0], moe_grad, back_rows[-1:], tuple(counts[-1:]), width
    )

    kv_sum, dq_back = hold((kv_sum, dq_back), prob_grad)
    query_grad = lax.dynamic_update_slice(query_grad, dq_back, (0, (1 - core) * half))
    factor = jnp.where(jnp.arange(2 * HEAD) < HEAD, F32(HEAD**-0.5), F32(1.0))
    summed = (kv_sum.astype(F32) * factor).astype(BF)
    tok = kv_rows.shape[0]
    kv_own, kv_back = summed[:tok], swap(summed[tok:])
    kv_grad = jnp.where(
        core == 0,
        jnp.concatenate([kv_own, kv_back], 1),
        jnp.concatenate([kv_back, kv_own], 1),
    )
    return moe_grad[None], prob_grad[None], query_grad[None], kv_grad[None]


def solution(mesh):
    tokens = P("exp", "ctx", None)
    placed = (
        tokens,
        tokens,
        tokens,
        P("ctx", "exp", None, None),
        P("exp", None, "ctx"),
        tokens,
        tokens,
        tokens,
        tokens,
        tokens,
    )
    return jax.shard_map(
        body,
        mesh=mesh,
        in_specs=placed,
        out_specs=(tokens, tokens, tokens, tokens),
        check_vma=False,
    )
```

```python
import functools

import jax
import jax.numpy as jnp
from jax import lax
from jax.experimental import pallas as pl
from jax.experimental.pallas import tpu as pltpu
from jax.sharding import PartitionSpec as P

HEAD = 128
BF, F32 = jnp.bfloat16, jnp.float32
LOG2E = 1.4426950408889634
GROUPS = ((0, 1, 2), (3, 4))
PARTS = (4, 4, 4, 4)
HOLD = {2: 1}


def mm(a, b, dims=((1,), (0,))):
    return lax.dot_general(a, b, (dims, ((), ())), preferred_element_type=F32)


def iota(shape, dim):
    return lax.broadcasted_iota(jnp.int32, shape, dim)


def as_bf(mask):
    return jnp.where(mask, 1.0, 0.0).astype(BF)


def params(mib=48, **kw):
    return pltpu.CompilerParams(vmem_limit_bytes=mib * 1024 * 1024, **kw)


def cost(flops, nbytes, exps=0):
    return pl.CostEstimate(flops=flops, bytes_accessed=nbytes, transcendentals=exps)


def dispatch_kernel(routes_ref, left_ref, right_ref, send_ref, mask_ref, turned):
    @pl.when(pl.program_id(0) == 0)
    def _():
        tok = routes_ref.shape[0]
        route = routes_ref[...]
        lane = iota((tok, tok), 1)
        hot = route == lane
        lower = iota((tok, tok), 0) > lane
        earlier = mm(as_bf(lower), as_bf(hot))
        slot = jnp.sum(jnp.where(hot, earlier, 0.0), axis=1, keepdims=True).astype(jnp.int32)
        first = jnp.where(slot < 8, route * 8 + slot, -1)
        second = jnp.where(slot < 8, -8, route * 8 + slot - 8)
        for i, key in enumerate((first, second, second + 4)):
            one = jnp.where(key == lane, 1.0, 0.0)
            mask_ref[i] = one.astype(BF)
            turned[i] = one.T.astype(BF)

    left, right = left_ref[...], right_ref[...]
    w = left.shape[1]
    send_ref[:, :w] = mm(turned[0], left).astype(BF)
    send_ref[:, w : 2 * w] = mm(turned[0], right).astype(BF)
    send_ref[:, 2 * w :] = (mm(turned[1], left) + mm(turned[2], right)).astype(BF)


def dispatch(routes, grad):
    tok, width = grad.shape
    steps = 4
    w = width // (2 * steps)
    return pl.pallas_call(
        dispatch_kernel,
        grid=(steps,),
        in_specs=[
            pl.BlockSpec((tok, 1), lambda j: (0, 0)),
            pl.BlockSpec((tok, w), lambda j: (0, j)),
            pl.BlockSpec((tok, w), lambda j: (0, j + steps)),
        ],
        out_specs=[
            pl.BlockSpec((tok, 3 * w), lambda j: (0, j)),
            pl.BlockSpec((3, tok, tok), lambda j: (0, 0, 0)),
        ],
        out_shape=[
            jax.ShapeDtypeStruct((tok, 3 * steps * w), BF),
            jax.ShapeDtypeStruct((3, tok, tok), BF),
        ],
        scratch_shapes=[pltpu.VMEM((3, tok, tok), BF)],
        compiler_params=params(dimension_semantics=("arbitrary",)),
        cost_estimate=cost(4 * tok * tok * width, 5 * tok * width),
        name="dispatch",
    )(routes, grad, grad)


def hidden_kernel(rows_ref, dl_ref, dr_ref, pre_ref, grad_ref, prob_ref, acc_l, acc_r):
    j = pl.program_id(0)
    half = rows_ref.shape[0]
    w = dl_ref.shape[1]
    hidden = dl_ref.shape[0]
    extra = rows_ref[:, 2 * w :]
    left = mm(jnp.concatenate([rows_ref[:, :w], extra], 0), dl_ref[...], ((1,), (1,)))
    right = mm(jnp.concatenate([rows_ref[:, w : 2 * w], extra], 0), dr_ref[...], ((1,), (1,)))

    @pl.when(j == 0)
    def _():
        acc_l[...] = left
        acc_r[...] = right

    @pl.when(j > 0)
    def _():
        acc_l[...] += left
        acc_r[...] += right

    @pl.when(j == pl.num_programs(0) - 1)
    def _():
        slots = pre_ref.shape[0]
        row = iota((2 * half, slots), 0)
        inner = row & (half - 1)
        group = inner >> 3
        source = group * 12 + jnp.where(row < half, inner & 7, 8 + (inner & 3))
        pick = as_bf(source == iota((2 * half, slots), 1))
        lane = iota((half, 128), 1)
        probs = jnp.zeros((half, 128), F32)
        for part in range(2):
            here = slice(part * half, (part + 1) * half)
            chosen = pick[here]
            gate = mm(chosen, pre_ref[:, :hidden])
            up = mm(chosen, pre_ref[:, hidden:])
            if part == 0:
                down = acc_l[here] + acc_r[here]
            else:
                low = (iota((half, hidden), 0) & 7) < 4
                mixed = jnp.where(low, acc_l[here], acc_r[here]).reshape(half // 8, 8, hidden)
                down = (mixed + pltpu.roll(mixed, 4, 1)).reshape(half, hidden)
            sigma = jax.nn.sigmoid(gate)
            swish = gate * sigma
            prob = jnp.sum(down * swish * up, axis=1, keepdims=True)
            probs = jnp.where(lane == part, prob, probs)
            grad_ref[here, :hidden] = (
                down * up * sigma * (1.0 + gate * (1.0 - sigma))
            ).astype(BF)
            grad_ref[here, hidden:] = (down * swish).astype(BF)
        prob_ref[...] = probs.astype(BF)


def hidden_grad(rows, down, pre):
    half = rows.shape[0]
    hidden, width = down.shape
    steps = 4
    w = width // (2 * steps)
    return pl.pallas_call(
        hidden_kernel,
        grid=(steps,),
        in_specs=[
            pl.BlockSpec((half, 3 * w), lambda j: (0, j)),
            pl.BlockSpec((hidden, w), lambda j: (0, j)),
            pl.BlockSpec((hidden, w), lambda j: (0, j + steps)),
            pl.BlockSpec(pre.shape, lambda j: (0, 0)),
        ],
        out_specs=[
            pl.BlockSpec((2 * half, 2 * hidden), lambda j: (0, 0)),
            pl.BlockSpec((half, 128), lambda j: (0, 0)),
        ],
        out_shape=[
            jax.ShapeDtypeStruct((2 * half, 2 * hidden), BF),
            jax.ShapeDtypeStruct((half, 128), BF),
        ],
        scratch_shapes=[pltpu.VMEM((2 * half, hidden), F32)] * 2,
        compiler_params=params(dimension_semantics=("arbitrary",)),
        cost_estimate=cost(4 * half * width * hidden, 2 * hidden * width),
        name="hidden_grad",
    )(rows, down, down, pre)


def columns_kernel(sizes, with_prob, *refs):
    grad_ref = refs[0]
    shards = refs[1 : 1 + sum(sizes)]
    out_ref = refs[-1]
    half = grad_ref.shape[0] // 2
    low = (iota((half, 128), 0) & 7) < 4
    at = 0
    for n, size in enumerate(sizes):
        parts = [r[...] for r in shards[at : at + size]]
        at += size
        shard = parts[0] if size == 1 else jnp.concatenate(parts, 0)
        out = mm(grad_ref[...], shard, ((1,), (1,)))
        out_ref[:, n * 384 : n * 384 + 256] = out[:half].astype(BF)
        out_ref[:, n * 384 + 256 : (n + 1) * 384] = jnp.where(
            low, out[half:, :128], out[half:, 128:]
        ).astype(BF)
    if with_prob:
        out_ref[:, len(sizes) * 384 :] = refs[-2][...]


def columns(grad, shards, prob):
    half = grad.shape[0] // 2
    sizes = tuple(len(s) for s in shards)
    flat = [r for s in shards for r in s]
    wide = 384 * len(shards) + (0 if prob is None else 128)
    rest = [] if prob is None else [prob]
    return pl.pallas_call(
        functools.partial(columns_kernel, sizes, prob is not None),
        out_shape=jax.ShapeDtypeStruct((half, wide), BF),
        compiler_params=params(),
        cost_estimate=cost(
            2 * grad.size * 256 * len(shards), 2 * (grad.size + 256 * grad.shape[1] * len(shards))
        ),
        name="columns",
    )(grad, *flat, *rest)


def combine_kernel(counts, first, ids_ref, mask_ref, gate_ref, *refs):
    if first:
        arrived, (out_ref, prob_ref) = refs[:-2], refs[-2:]
    else:
        before, arrived, out_ref = refs[0], refs[1:-1], refs[-1]
        out_ref[...] = before[...]
    main_mask, low, high = mask_ref[0], mask_ref[1], mask_ref[2]
    gate = gate_ref[...]
    place = 0
    for ref, count in zip(arrived, counts):
        for k in range(count):
            main = ref[:, k * 384 : k * 384 + 256]
            extra = ref[:, k * 384 + 256 : (k + 1) * 384]
            picked = mm(main_mask, main) + jnp.concatenate([mm(low, extra), mm(high, extra)], 1)
            where = pl.multiple_of(ids_ref[place] * 256, 256)
            out_ref[:, pl.ds(where, 256)] = (gate * picked).astype(BF)
            place += 1
    if first:
        probs = arrived[0][:, counts[0] * 384 :]
        prob_ref[...] = (mm(main_mask, probs)[:, :1] + mm(low, probs)[:, 1:2]).astype(BF)


def combine(ids, masks, gate, before, arrived, counts, width):
    tok = gate.shape[0]
    first = before is None
    vmem = pl.BlockSpec(memory_space=pltpu.VMEM)
    operands = ([] if first else [before]) + list(arrived)
    out_shape = [jax.ShapeDtypeStruct((tok, width), BF)]
    if first:
        out_shape.append(jax.ShapeDtypeStruct((tok, 1), BF))
    return pl.pallas_call(
        functools.partial(combine_kernel, counts, first),
        in_specs=[pl.BlockSpec(memory_space=pltpu.SMEM)] + [vmem] * (2 + len(operands)),
        out_specs=[vmem] * len(out_shape),
        out_shape=out_shape,
        compiler_params=params(),
        cost_estimate=cost(4 * tok * tok * 256 * sum(counts), 6 * tok * width),
        name="combine",
    )(ids, masks, gate, *operands)


def delta_kernel(grad_ref, out_ref, delta_ref):
    heads = delta_ref.shape[0]
    for h in range(heads):
        cols = slice(h * HEAD, (h + 1) * HEAD)
        product = grad_ref[:, cols].astype(F32) * out_ref[:, cols].astype(F32)
        delta_ref[h : h + 1, :] = jnp.sum(product.T, axis=0, keepdims=True)


def deltas(grad, out):
    tok, width = grad.shape
    return pl.pallas_call(
        delta_kernel,
        out_shape=jax.ShapeDtypeStruct((width // HEAD, tok), F32),
        compiler_params=params(),
        cost_estimate=cost(2 * tok * width, 4 * tok * width),
        name="deltas",
    )(grad, out)


def attend_kernel(first, last, pairs, start, place_ref, *refs):
    q_ref, g_ref, qo_ref, go_ref, d_ref, do_ref = refs[:6]
    kv = refs[6:14]
    at = 14
    if not first:
        turned, before = refs[at : at + 2]
        at += 4
    dq_ref, dqo_ref = refs[at : at + 2]
    at += 2
    if first:
        turned = refs[at]
        at += 1
    if last:
        sent_ref = refs[at]
        at += 1
    sums, kept, low_probs, low_grads = refs[at : at + 4]
    i = pl.program_id(0)
    chip, core = place_ref[0], place_ref[1]
    tok = q_ref.shape[0]
    block = 2 * tok
    rows = 2 * block
    scale = HEAD**-0.5
    factor = scale * LOG2E
    n_heads = do_ref.shape[0]
    valid = [None] + [chip >= s for s in range(1, 5)] + [chip + s >= 8 for s in range(1, 4)]

    @pl.when(i == 0)
    def _():
        if first:
            sums[...] = jnp.zeros_like(sums)
            for s in range(8):
                turned[:, s * block : (s + 1) * block] = kv[s][:, :HEAD].T
        else:
            sums[...] = before[...]

    def stack(own, other):
        return jnp.concatenate(
            [own[:, :HEAD], other[:, :HEAD], own[:, HEAD:], other[:, HEAD:]], 0
        )

    query = stack(q_ref, qo_ref)
    grad = stack(g_ref, go_ref)
    head = start + 2 * i
    delta = jnp.concatenate(
        [
            r[pl.ds(at_head, 1), :]
            for n in range(2)
            for r, at_head in ((d_ref, core * n_heads + head + n), (do_ref, head + n))
        ],
        1,
    )
    highest = total = None
    bases = []
    for s in range(8):
        here = slice(s * block, (s + 1) * block)
        scores = mm(kv[s][:, :HEAD], query, ((1,), (1,)))
        if s == 0:
            flip = core * tok
            key_pos = iota((block, rows), 0) ^ flip
            row_pos = (iota((block, rows), 1) & (block - 1)) ^ flip
            scores = jnp.where(key_pos <= row_pos, scores, -1e30)
        top = jnp.max(scores, axis=0, keepdims=True)
        if s == 0:
            new = base = top
        else:
            new = jnp.maximum(highest, jnp.where(valid[s], top, -1e30))
            base = jnp.where(valid[s], new, 1e30)
        expo = jnp.exp2((scores - base) * factor)
        kept[here, :] = expo
        fresh = jnp.sum(expo, axis=0, keepdims=True)
        total = fresh if s == 0 else total * jnp.exp2((highest - new) * factor) + fresh
        highest = new
        bases.append(new)
    inverse = 1.0 / total
    for s in range(8):
        here = slice(s * block, (s + 1) * block)
        share = inverse * jnp.exp2((bases[s] - highest) * factor)
        probs = kept[here, :] * share
        part = mm(kv[s][:, HEAD:], grad, ((1,), (1,)))
        low_grads[here, :] = (probs * (part - delta)).astype(BF)
        low_probs[here, :] = probs.astype(BF)
    sums[:, HEAD:] += mm(low_probs[...], grad)
    sums[:, :HEAD] += mm(low_grads[...], query)
    dq = (mm(turned[...], low_grads[...]) * scale).T.astype(BF)
    for n in range(2):
        cols = slice(n * HEAD, (n + 1) * HEAD)
        dq_ref[:, cols] = dq[n * block : n * block + tok]
        dqo_ref[:, cols] = dq[n * block + tok : (n + 1) * block]

    if last:

        @pl.when(i == pairs - 1)
        def _():
            for s in range(8):
                source = lax.rem(chip + (8 - s if s < 5 else s - 4), 8)
                to = pl.ds(pl.multiple_of(source * block, block), block)
                sent_ref[to, :] = sums[s * block : (s + 1) * block, :]


def attend(first, last, start, heads, place, queries, grads, others, delta, delta_other, kv, carry):
    tok, width = queries.shape
    n_heads = width // HEAD // 2
    pairs = heads // 2
    pair = (tok, 2 * HEAD)
    block, rows = 2 * tok, 4 * tok
    lead = start // 2

    def whole(a):
        return pl.BlockSpec(a.shape, lambda i, p: (0,) * len(a.shape))

    half_pairs = n_heads // 2
    sums = jax.ShapeDtypeStruct((8 * block, 2 * HEAD), F32)
    turned = jax.ShapeDtypeStruct((HEAD, 8 * block), BF)
    out_shape = [
        jax.ShapeDtypeStruct((tok, width), BF),
        jax.ShapeDtypeStruct((tok, width // 2), BF),
    ]
    out_specs = [
        pl.BlockSpec(pair, lambda i, p: (0, p[1] * half_pairs + lead + i)),
        pl.BlockSpec(pair, lambda i, p: (0, lead + i)),
    ]
    scratch = [
        pltpu.VMEM((8 * block, rows), F32),
        pltpu.VMEM((8 * block, rows), BF),
        pltpu.VMEM((8 * block, rows), BF),
    ]
    extra = []
    if first:
        extra.append(turned)
    if last:
        extra.append(sums)
        scratch = [pltpu.VMEM(sums.shape, F32)] + scratch
    else:
        extra.append(sums)
    mine = pl.BlockSpec(pair, lambda i, p: (0, p[1] * half_pairs + lead + i))
    in_specs = [
        mine,
        mine,
        pl.BlockSpec(pair, lambda i, p: (0, lead + i)),
        pl.BlockSpec(pair, lambda i, p: (0, half_pairs + lead + i)),
        whole(delta),
        whole(delta_other),
    ]
    in_specs += [whole(a) for a in kv]
    more = list(kv)
    alias = {}
    if not first:
        in_specs += [whole(a) for a in carry[:2]] + [pl.BlockSpec(memory_space=pl.ANY)] * 2
        more += list(carry)
        alias = {17: 0, 18: 1}
    return pl.pallas_call(
        functools.partial(attend_kernel, first, last, pairs, start),
        grid_spec=pltpu.PrefetchScalarGridSpec(
            num_scalar_prefetch=1,
            grid=(pairs,),
            in_specs=in_specs,
            out_specs=out_specs + [whole(a) for a in extra],
            scratch_shapes=scratch,
        ),
        out_shape=out_shape + extra,
        input_output_aliases=alias,
        compiler_params=params(60, dimension_semantics=("arbitrary",)),
        cost_estimate=cost(
            40 * heads * 8 * block * block * HEAD, 12 * tok * width, heads * 8 * block * block
        ),
        name="attend",
    )(place, queries, grads, others, others, delta, delta_other, *more)


def hold(x, until):
    return lax.optimization_barrier((x, until))[0]


def along(x, step):
    return lax.ppermute(x, "ctx", [(i, (i + 2 * step) % 16) for i in range(16)])


def swap(x):
    return lax.ppermute(x, "ctx", [(i, i ^ 1) for i in range(16)])


def exchange(x):
    groups = lax.axis_size("exp")
    cut = x.reshape(groups, x.shape[0] // groups, x.shape[1])
    out = lax.all_to_all(cut, "exp", split_axis=0, concat_axis=0, tiled=True)
    return out.reshape(x.shape)


def body(
    grad_out,
    routes,
    gate_probs,
    saved_pre,
    down_weight,
    gate_up_weight,
    queries,
    keys_values,
    attn_grad,
    attn_out,
):
    width = grad_out.shape[2]
    index = lax.axis_index("ctx")
    chip, core = index // 2, index % 2
    place = jnp.stack([chip, core]).astype(jnp.int32)
    query, grad, kv_rows = queries[0], attn_grad[0], keys_values[0]
    half = width // 2

    def mine(x, n):
        return lax.dynamic_slice_in_dim(x, core * n, n, 1)

    def theirs(x, n):
        return lax.dynamic_slice_in_dim(x, (1 - core) * n, n, 1)

    own = jnp.concatenate([mine(kv_rows, 2 * HEAD), swap(theirs(kv_rows, 2 * HEAD))], 0)
    up, down = [own], [own]
    for s in range(4):
        up.append(along(up[-1], 1))
        if s < 3:
            down.append(along(down[-1], -1))
    kv = up + down[1:]

    send, masks = dispatch(routes[0], grad_out[0])
    arrived = exchange(send)

    full_down = lax.all_gather(down_weight[0], "ctx", axis=1, tiled=True)
    shard = gate_up_weight[0]
    begin = hold(shard, (up[3], down[3]))
    fore, back = [begin], [begin]
    fore.append(along(begin, 1))
    back.append(along(begin, -1))

    delta = deltas(grad, attn_out[0])
    query_late, grad_late = hold((query, grad), up[0])
    others = swap(jnp.concatenate([theirs(query_late, half), theirs(grad_late, half)], 1))
    n_heads = delta.shape[0] // 2
    delta_other = swap(lax.dynamic_slice_in_dim(delta, (1 - core) * n_heads, n_heads, 0))
    carry = None
    for n, heads in enumerate(PARTS):
        begun, ended = n == 0, n == len(PARTS) - 1
        operands = (query, grad, others, delta, delta_other)
        if n == 0:
            operands = hold(operands, send)
        if n == 2:
            fore[1], back[1] = hold((fore[1], back[1]), outs[-1])
            for s in range(2):
                fore.append(along(fore[-1], 1))
                back.append(along(back[-1], -1))
            mid = shard.shape[0] // 2
            last = (along(fore[3][:mid], 1), along(back[3][mid:], -1))
            steps = [[((shard,), chip, core), ((swap(shard),), chip, 1 - core)]]
            for s in range(1, 4):
                steps.append(
                    [
                        ((fore[s],), chip - s, core),
                        ((back[s],), chip + s, core),
                        ((swap(fore[s]),), chip - s, 1 - core),
                        ((swap(back[s]),), chip + s, 1 - core),
                    ]
                )
            steps.append(
                [(last, chip + 4, core), (tuple(swap(x) for x in last), chip + 4, 1 - core)]
            )
        if ended:
            operands = hold(operands, arrived)
        if n in HOLD:
            operands = hold(operands, (fore[HOLD[n]], back[HOLD[n]]))
        outs = attend(begun, ended, sum(PARTS[:n]), heads, place, *operands, kv, carry)
        if begun:
            turned = outs[2]
        carry = (turned, outs[-1], outs[0], outs[1])
    query_grad, dq_other = outs[:2]
    terms = outs[-1]
    dq_back = swap(dq_other)
    chips = [[2 * z + c for z in range(8)] for c in range(2)]
    kv_sum = lax.psum_scatter(
        hold(terms, (fore[3], back[3])), "ctx", scatter_dimension=0, tiled=True, axis_index_groups=chips
    )

    arrived = hold(arrived, terms)
    hidden, prob = hidden_grad(arrived, full_down, saved_pre[0, 0])
    back_rows, counts, ids = [], [], []
    for n, group in enumerate(GROUPS):
        members = [m for s in group for m in steps[s]]
        source = hidden
        if n == 0:
            source = hold(hidden, (fore[3], back[3]))
        if n == 1:
            source = hold(hidden, out)
        out = columns(source, [m[0] for m in members], prob if n == 0 else None)
        if n == 0:
            out = hold(out, last)
        back_rows.append(exchange(out))
        counts.append(len(members))
        ids.append(
            jnp.stack([((m[1] + 8) % 8) * 2 + m[2] for m in members]).astype(jnp.int32)
        )
    moe_grad, prob_grad = combine(
        jnp.concatenate(ids[:-1]), masks, gate_probs[0], None, back_rows[:-1], tuple(counts[:-1]), width
    )
    (moe_grad,) = combine(
        ids[-1], masks, gate_probs[0], moe_grad, back_rows[-1:], tuple(counts[-1:]), width
    )

    kv_sum, dq_back = hold((kv_sum, dq_back), prob_grad)
    query_grad = lax.dynamic_update_slice(query_grad, dq_back, (0, (1 - core) * half))
    factor = jnp.where(jnp.arange(2 * HEAD) < HEAD, F32(HEAD**-0.5), F32(1.0))
    summed = (kv_sum.astype(F32) * factor).astype(BF)
    tok = kv_rows.shape[0]
    kv_own, kv_back = summed[:tok], swap(summed[tok:])
    kv_grad = jnp.where(
        core == 0,
        jnp.concatenate([kv_own, kv_back], 1),
        jnp.concatenate([kv_back, kv_own], 1),
    )
    return moe_grad[None], prob_grad[None], query_grad[None], kv_grad[None]


def solution(mesh):
    tokens = P("exp", "ctx", None)
    placed = (
        tokens,
        tokens,
        tokens,
        P("ctx", "exp", None, None),
        P("exp", None, "ctx"),
        tokens,
        tokens,
        tokens,
        tokens,
        tokens,
    )
    return jax.shard_map(
        body,
        mesh=mesh,
        in_specs=placed,
        out_specs=(tokens, tokens, tokens, tokens),
        check_vma=False,
    )
```
